32 devices in a mesh: groups: 2 (over x), dp: 16 (over z, y, core), tensor: 1.
Axes of the slice: x: 2, y: 2, z: 4, core: 2. Of those that a mesh axis runs over, the one named last changes fastest.
Arguments:
- doc_hidden: bfloat16 [1280, 32, 4096], P(('groups', 'dp'), None, 'tensor'), parts along dimension 0, may hold values from -6 to 6
- proj_weight: bfloat16 [4096, 128], P('tensor'), may hold values from -0.09375 to 0.09375
- query_reps: bfloat16 [32, 32, 128], P(('groups', 'dp')), parts along dimension 0, may hold values from -6 to 6
- teacher: float32 [32, 256], P(('groups', 'dp')), parts along dimension 0, may hold values from -0.4 to 0.4
- cand_peer: int32 [32, 256, 1], P(('groups', 'dp')), parts along dimension 0, may hold values from 0 to 15; in each aligned block of 256 rows (0 to 255, 256 to 511, ..., all dimensions but the last counted through in order) at most 32 rows name the same one
- cand_doc: int32 [32, 256], P(('groups', 'dp')), parts along dimension 0, may hold values from 0 to 39
- tile_count: int32 [32], P(('groups', 'dp')), parts along dimension 0, may hold values from 1 to 2
- doc_len: int32 [1280], P('groups'), parts along dimension 0, may hold values from 1 to 32
Outputs:
- grad_hidden: bfloat16 [1280, 32, 4096], P(('groups', 'dp'), None, 'tensor'), parts along dimension 0
- grad_weight: float32 [8192, 128], P(('groups', 'tensor')), parts along dimension 0
- grad_query: float32 [32, 32, 128], P(('groups', 'dp')), parts along dimension 0
The draws below stay inside these ranges and needn't reach their ends.
There are 2 independent parts, one for each index of `groups`. The reference program is written for one: setup_inputs(seed, part) draws one part's arguments, and reference() takes and returns one part's arrays. A program takes and returns all parts, laid end to end along the dimension named above; an argument that names none is the same for every part. Nothing has to cross between parts.
Inputs may be any that keep to these rules, and one draw needn't show every extreme that they name: `cand_peer`: in each aligned block of 256 slots (the queries of one dp index) no shard is named more than 32 times; in some block some shard is named exactly 32 times.
All inputs are finite; a program needn't handle non-finite values.
Results may differ from the reference program's by a relative error of at most 0.0077.
Values may be sent and summed in bfloat16 or wider, within the bound.
A program may use at most 128 MiB of HBM per device.

```python
import math
import jax
import jax.numpy as jnp
import numpy as np
from jax import lax

HID = 4096
EMB = 128
QT = 32
DT = 32
TILE = 128
MAXT = 2
Q_DEV = 1
ENC_DEV = 40
SLOTS = 256
SHARDS = 16
CAP = 32
QUERIES = 16
DOCS = 640


def draw_doc_len(key, part):
    key = jax.random.fold_in(key, 11)
    flag_key, short_key = jax.random.split(key)
    full_flag = jax.random.randint(flag_key, (DOCS,), 0, 2)
    short_len = jax.random.randint(short_key, (DOCS,), 1, DT // 4 + 1)
    return jnp.where(full_flag == 1, DT, short_len).astype(jnp.int32)


def with_ends(drawn, own_key, least, top_value):
    place = [jax.random.randint(jax.random.fold_in(own_key, axis), (), 0, length) for axis, length in enumerate(drawn.shape)]
    main_axis = drawn.shape.index(max(drawn.shape))
    neighbour = place[:main_axis] + [(place[main_axis] + 1) % drawn.shape[main_axis]] + place[main_axis + 1:]
    return drawn.at[tuple(place)].set(least).at[tuple(neighbour)].set(top_value)


def steps_of(own_key, dims, cuts, low, high):
    level = 1.0
    for axis_at, blocks in cuts:
        draws = jax.random.uniform(jax.random.fold_in(jax.random.fold_in(own_key, 6), axis_at), (blocks,), jnp.float32, low / len(cuts), high / len(cuts))
        level = level * jnp.repeat(jnp.exp(draws), dims[axis_at] // blocks).reshape((-1,) + (1,) * (len(dims) - 1 - axis_at))
    return level


def routed_block(stream_key, own, number, rows, number_of, top, bound, lean):
    ranking = jax.random.permutation(stream_key, number_of)
    packed, common = shares(number_of, rows * top, bound, lean, True), shares(number_of, rows * top, bound, lean, False)
    places = jnp.arange(number_of)

    def named(tallies, turn):
        used = int((tallies > 0).sum())
        fixed = max(1, used // 4)
        moved = fixed + (places - fixed + turn * (used - fixed)) % max(1, number_of - fixed)
        return jnp.zeros((number_of,), jnp.int32).at[ranking[jnp.where(places < fixed, places, moved)]].set(jnp.asarray(tallies, jnp.int32))

    tallies = jnp.where(number % 4 == 0, named(packed, number // 4), named(common, number - number // 4 - 1))
    mixed = jax.random.permutation(jax.random.fold_in(own, 3), number_of)
    source_of, taker = mixed[0:number_of // 2 * 2:2], mixed[1:number_of // 2 * 2:2]
    margin = jnp.minimum(tallies[source_of] - 1, bound - tallies[taker]) // 2
    margin = jnp.where((source_of == ranking[0]) | (taker == ranking[0]) | (tallies[taker] == 0), 0, jnp.maximum(margin, 0))
    moved = jax.random.randint(jax.random.fold_in(own, 4), (number_of // 2,), 0, 1 << 20) % (margin + 1)
    tallies = tallies.at[source_of].add(-moved).at[taker].add(moved)
    members = jnp.searchsorted(jnp.cumsum(tallies), jnp.arange(rows * top), side="right").astype(jnp.int32)
    listing = members.reshape(top, rows).T
    listing = listing[jax.random.permutation(jax.random.fold_in(own, 1), rows)]
    turn = jax.random.randint(jax.random.fold_in(own, 2), (rows, 1), 0, top)
    return jnp.take_along_axis(listing, (jnp.arange(top)[None, :] + turn) % top, axis=1)


def shares(number_of, total, limit, skew, full):
    weights = [(1 << 20) // math.isqrt(rank ** skew) + 1 for rank in range(1, number_of + 1)]
    largest = limit if full else min(limit, max(-(-total // number_of), total * weights[0] // sum(weights)))
    least = 1 if total - largest >= number_of - 1 else 0
    counts, surplus = [largest] + [least] * (number_of - 1), total - largest - least * (number_of - 1)
    while surplus > 0:
        free = [i for i in range(1, number_of) if counts[i] < largest] or [i for i in range(1, number_of) if counts[i] < limit]
        pool, left = sum([weights[i] for i in free]), surplus
        for i in free:
            extra = min(limit - counts[i], max(1, left * weights[i] // pool), surplus)
            counts[i] = counts[i] + extra
            surplus = surplus - extra
    return np.array(counts)


def centred(stream_key, dims, deviation, bound, cuts=(), kind=jnp.bfloat16):
    values = jax.random.normal(stream_key, dims, jnp.float32) * deviation
    if len(cuts) > 0:
        values = steps_of(stream_key, dims, cuts, -0.22, 0.18) * values
    return jnp.clip(values, min=-bound, max=bound).astype(kind)


def setup_inputs(seed: int = 0, part: int = 0) -> dict:
    seeds = jax.random.split(jax.random.key(seed), 9)
    part_keys = jax.random.split(jax.random.fold_in(seeds[8], part), 9)
    doc_hidden = centred(part_keys[0], (DOCS, DT, HID), 1.0, 6.0, ((0, 16),))
    proj_weight = centred(seeds[1], (HID, EMB), HID ** -0.5, 0.09375)
    query_reps = centred(part_keys[2], (QUERIES, QT, EMB), 1.0, 6.0, ((0, 16),))
    teacher = jnp.clip(jax.random.uniform(part_keys[3], (QUERIES, SLOTS), jnp.float32, -0.4, 0.4) * steps_of(part_keys[3], (QUERIES, SLOTS), ((0, 16),), -0.4, 0.0), -0.4, 0.4)
    cand_peer_keys = jax.random.split(jax.random.fold_in(part_keys[4], 1), QUERIES * SLOTS // (Q_DEV * SLOTS))
    cand_peer_turns = jax.random.permutation(jax.random.fold_in(part_keys[4], 3), QUERIES * SLOTS // (Q_DEV * SLOTS))
    cand_peer = jax.vmap(lambda own, number: routed_block(jax.random.fold_in(part_keys[4], 2), own, number, Q_DEV * SLOTS, SHARDS, 1, CAP, 2))(cand_peer_keys, cand_peer_turns).reshape((QUERIES, SLOTS, 1))
    cand_doc = with_ends(jax.random.randint(part_keys[5], (QUERIES, SLOTS), 0, ENC_DEV), jax.random.fold_in(part_keys[5], 1), 0, ENC_DEV - 1).astype(jnp.int32)
    tile_count = with_ends(jax.random.randint(part_keys[6], (QUERIES,), 1, MAXT + 1), jax.random.fold_in(part_keys[6], 1), 1, MAXT).astype(jnp.int32)
    doc_len = draw_doc_len(jax.random.fold_in(jax.random.fold_in(seeds[8], part), 71), part)
    return {"doc_hidden": doc_hidden, "proj_weight": proj_weight, "query_reps": query_reps, "teacher": teacher, "cand_peer": cand_peer, "cand_doc": cand_doc, "tile_count": tile_count, "doc_len": doc_len}


token_temp = 0.5
list_temp = 0.2
loss_scale = 4096.0
epsilon = 1e-06

def unit_rows(values):
    factor = lax.rsqrt(lax.optimization_barrier(jnp.mean(values * values, axis=-1, keepdims=True)) + epsilon)
    return (values * factor, factor)

def reference(doc_hidden, proj_weight, query_reps, teacher, cand_peer, cand_doc, tile_count, doc_len):
    flat_hidden = doc_hidden.reshape(DOCS * DT, HID)
    doc_proj = jnp.dot(flat_hidden, proj_weight, preferred_element_type=jnp.float32).reshape(DOCS, DT, EMB)
    doc_unit, doc_factor = unit_rows(doc_proj)
    doc_narrow = doc_unit.astype(jnp.bfloat16)
    query_unit, query_factor = unit_rows(query_reps.astype(jnp.float32))
    query_narrow = query_unit.astype(jnp.bfloat16)
    doc_ids = (cand_peer[:, :, 0] * ENC_DEV + cand_doc).astype(jnp.int32)
    slot_valid = ((jnp.arange(SLOTS) // TILE)[None, :] < tile_count[:, None]).astype(jnp.float32)
    inv_root = 1.0 / math.sqrt(EMB)

    def forward_query(inputs):
        query_rows, chosen = inputs
        doc_rows = doc_narrow[chosen]
        token_mask = (jnp.arange(DT)[None, :] < doc_len[chosen][:, None]).astype(jnp.float32)
        similarity = jnp.einsum('id,sjd->sij', query_rows.astype(jnp.float32), doc_rows.astype(jnp.float32)) * inv_root
        weights = jnp.exp(similarity / token_temp) * token_mask[:, None, :]
        return (weights, lax.optimization_barrier(jnp.sum(weights, axis=-1)))
    weights, totals = lax.map(forward_query, (query_narrow, doc_ids))
    maxsim = token_temp * jnp.log(totals)
    scores = lax.optimization_barrier(jnp.mean(maxsim, axis=-1))
    student = jnp.exp(scores / list_temp) * slot_valid
    student = student / lax.optimization_barrier(jnp.sum(student, axis=-1, keepdims=True))
    target = jnp.exp(teacher) * slot_valid
    target = target / lax.optimization_barrier(jnp.sum(target, axis=-1, keepdims=True))
    score_grad = loss_scale * (student - target) / list_temp

    def backward_query(running, inputs):
        query_rows, chosen, query_weights, query_totals, query_score_grad = inputs
        doc_rows = doc_narrow[chosen]
        token_grad = query_weights / query_totals[..., None] * (query_score_grad / QT)[:, None, None]
        token_narrow = token_grad.astype(jnp.bfloat16).astype(jnp.float32)
        unit_grad = jnp.einsum('sij,id->sjd', token_narrow, query_rows.astype(jnp.float32)) * inv_root
        query_part = jnp.einsum('sij,sjd->id', token_narrow, doc_rows.astype(jnp.float32)) * inv_root
        return (running.at[chosen].add(unit_grad), query_part)
    doc_grad, query_sum = lax.scan(backward_query, jnp.zeros((DOCS, DT, EMB), jnp.float32), (query_narrow, doc_ids, weights, totals, score_grad))
    proj_grad = doc_factor * (doc_grad - doc_unit * lax.optimization_barrier(jnp.mean(doc_unit * doc_grad, axis=-1, keepdims=True)))
    proj_narrow = proj_grad.astype(jnp.bfloat16).reshape(DOCS * DT, EMB)
    grad_hidden = jnp.dot(proj_narrow, proj_weight.T, preferred_element_type=jnp.float32).astype(jnp.bfloat16).reshape(DOCS, DT, HID)
    grad_weight = jnp.dot(flat_hidden.T, proj_narrow, preferred_element_type=jnp.float32) / DOCS
    grad_query = query_factor * (query_sum - query_unit * lax.optimization_barrier(jnp.mean(query_unit * query_sum, axis=-1, keepdims=True)))
    return (grad_hidden, grad_weight, grad_query)
```

```python
import math

import jax
import jax.numpy as jnp
from jax import lax
from jax.sharding import PartitionSpec as P

EMB = 128
QT = 32
TILE = 128

token_temp = 0.5
list_temp = 0.2
loss_scale = 4096.0
epsilon = 1e-06


def unit_rows(values):
    factor = lax.rsqrt(jnp.mean(values * values, axis=-1, keepdims=True) + epsilon)
    return (values * factor, factor)


def list_tables(teacher, cand_peer, cand_doc, tile_count, shards, enc_count):
    slot_count = cand_doc.shape[1]
    valid = (jnp.arange(slot_count)[None, :] // TILE < tile_count[:, None]).astype(jnp.float32)
    target = jnp.exp(teacher) * valid
    target = target / jnp.sum(target, axis=-1, keepdims=True)
    ident = cand_peer[:, :, 0] * enc_count + cand_doc
    named = ident[:, :, None] == jnp.arange(shards * enc_count, dtype=jnp.int32)[None, None, :]
    count = jnp.sum(jnp.where(named, valid[:, :, None], 0.0), axis=1)
    wanted = jnp.sum(jnp.where(named, target[:, :, None], 0.0), axis=1)
    return count, wanted


def with_collectives(
    doc_hidden, proj_weight, query_reps, teacher, cand_peer, cand_doc, tile_count, doc_len
):
    enc_count, doc_tokens, hidden_part = doc_hidden.shape
    shards = lax.axis_size("dp")
    me = lax.axis_index("dp")
    inv_root = 1.0 / math.sqrt(EMB)
    query_unit, query_factor = unit_rows(query_reps.astype(jnp.float32))
    query_narrow = query_unit.astype(jnp.bfloat16)
    count, wanted = list_tables(teacher, cand_peer, cand_doc, tile_count, shards, enc_count)
    every_query = lax.all_gather(query_narrow, "dp", axis=0, tiled=True)
    tables = lax.all_gather(jnp.stack([count, wanted], axis=1), "dp", axis=0, tiled=True)
    tables = lax.dynamic_slice_in_dim(tables, me * enc_count, enc_count, axis=2)
    count, wanted = tables[:, 0], tables[:, 1]
    flat_hidden = doc_hidden.reshape(enc_count * doc_tokens, hidden_part)
    proj_part = jnp.dot(flat_hidden, proj_weight, preferred_element_type=jnp.float32)
    doc_proj = lax.psum(proj_part, "tensor").reshape(enc_count, doc_tokens, EMB)
    doc_unit, doc_factor = unit_rows(doc_proj)
    doc_narrow = doc_unit.astype(jnp.bfloat16)
    own_len = lax.dynamic_slice_in_dim(doc_len, me * enc_count, enc_count)
    token_mask = (jnp.arange(doc_tokens)[None, :] < own_len[:, None]).astype(jnp.float32)
    similarity = (
        jnp.einsum("qid,ejd->qiej", every_query, doc_narrow, preferred_element_type=jnp.float32)
        * inv_root
    )
    weights = jnp.exp(similarity / token_temp) * token_mask
    totals = jnp.sum(weights, axis=-1)
    scores = jnp.mean(token_temp * jnp.log(totals), axis=1)
    raised = jnp.exp(scores / list_temp) * count
    norm = lax.psum(jnp.sum(raised, axis=-1), "dp")
    score_grad = loss_scale * (raised / norm[:, None] - wanted) / list_temp
    token_grad = weights / totals[..., None] * (score_grad / QT)[:, None, :, None]
    token_narrow = token_grad.astype(jnp.bfloat16)
    doc_grad = (
        jnp.einsum("qiej,qid->ejd", token_narrow, every_query, preferred_element_type=jnp.float32)
        * inv_root
    )
    query_part = (
        jnp.einsum("qiej,ejd->qid", token_narrow, doc_narrow, preferred_element_type=jnp.float32)
        * inv_root
    )
    query_sum = lax.psum_scatter(query_part, "dp", scatter_dimension=0, tiled=True)
    proj_grad = doc_factor * (
        doc_grad - doc_unit * jnp.mean(doc_unit * doc_grad, axis=-1, keepdims=True)
    )
    proj_narrow = proj_grad.astype(jnp.bfloat16).reshape(enc_count * doc_tokens, EMB)
    grad_hidden = lax.dot_general(
        proj_narrow, proj_weight, (((1,), (1,)), ((), ())), preferred_element_type=jnp.float32
    ).astype(jnp.bfloat16)
    grad_hidden = grad_hidden.reshape(enc_count, doc_tokens, hidden_part)
    weight_part = lax.dot_general(
        flat_hidden, proj_narrow, (((0,), (0,)), ((), ())), preferred_element_type=jnp.float32
    )
    grad_weight = lax.psum(weight_part, "dp") / (enc_count * shards)
    grad_query = query_factor * (
        query_sum - query_unit * jnp.mean(query_unit * query_sum, axis=-1, keepdims=True)
    )
    return (grad_hidden, grad_weight, grad_query)


def solution(mesh):
    placed = (
        P(("groups", "dp"), None, "tensor"),
        P("tensor", None),
        P(("groups", "dp"), None, None),
        P(("groups", "dp"), None),
        P(("groups", "dp"), None, None),
        P(("groups", "dp"), None),
        P(("groups", "dp")),
        P("groups"),
    )
    return jax.shard_map(
        with_collectives,
        mesh=mesh,
        in_specs=placed,
        out_specs=(
            P(("groups", "dp"), None, "tensor"),
            P(("groups", "tensor"), None),
            P(("groups", "dp"), None, None),
        ),
        check_vma=False,
    )
```

```python
import functools
import math

import jax
import jax.numpy as jnp
from jax import lax
from jax.experimental import pallas as pl
from jax.experimental.pallas import tpu as pltpu
from jax.sharding import PartitionSpec as P

EMB = 128
QT = 32
TILE = 128

token_temp = 0.5
list_temp = 0.2
loss_scale = 4096.0
epsilon = 1e-06


def unit_rows(values):
    factor = lax.rsqrt(jnp.mean(values * values, axis=-1, keepdims=True) + epsilon)
    return (values * factor, factor)


def list_tables(teacher, cand_peer, cand_doc, tile_count, shards, enc_count):
    slot_count = cand_doc.shape[1]
    valid = (jnp.arange(slot_count)[None, :] // TILE < tile_count[:, None]).astype(jnp.float32)
    target = jnp.exp(teacher) * valid
    target = target / jnp.sum(target, axis=-1, keepdims=True)
    ident = cand_peer[:, :, 0] * enc_count + cand_doc
    named = ident[:, :, None] == jnp.arange(shards * enc_count, dtype=jnp.int32)[None, None, :]
    count = jnp.sum(jnp.where(named, valid[:, :, None], 0.0), axis=1)
    wanted = jnp.sum(jnp.where(named, target[:, :, None], 0.0), axis=1)
    return count, wanted


def with_collectives(
    doc_hidden, proj_weight, query_reps, teacher, cand_peer, cand_doc, tile_count, doc_len
):
    enc_count, doc_tokens, hidden_part = doc_hidden.shape
    shards = lax.axis_size("dp")
    me = lax.axis_index("dp")
    inv_root = 1.0 / math.sqrt(EMB)
    query_unit, query_factor = unit_rows(query_reps.astype(jnp.float32))
    query_narrow = query_unit.astype(jnp.bfloat16)
    count, wanted = list_tables(teacher, cand_peer, cand_doc, tile_count, shards, enc_count)
    every_query = lax.all_gather(query_narrow, "dp", axis=0, tiled=True)
    tables = lax.all_gather(jnp.stack([count, wanted], axis=1), "dp", axis=0, tiled=True)
    tables = lax.dynamic_slice_in_dim(tables, me * enc_count, enc_count, axis=2)
    count, wanted = tables[:, 0], tables[:, 1]
    flat_hidden = doc_hidden.reshape(enc_count * doc_tokens, hidden_part)
    proj_part = jnp.dot(flat_hidden, proj_weight, preferred_element_type=jnp.float32)
    doc_proj = lax.psum(proj_part, "tensor").reshape(enc_count, doc_tokens, EMB)
    doc_unit, doc_factor = unit_rows(doc_proj)
    doc_narrow = doc_unit.astype(jnp.bfloat16)
    own_len = lax.dynamic_slice_in_dim(doc_len, me * enc_count, enc_count)
    token_mask = (jnp.arange(doc_tokens)[None, :] < own_len[:, None]).astype(jnp.float32)
    similarity = (
        jnp.einsum("qid,ejd->qiej", every_query, doc_narrow, preferred_element_type=jnp.float32)
        * inv_root
    )
    weights = jnp.exp(similarity / token_temp) * token_mask
    totals = jnp.sum(weights, axis=-1)
    scores = jnp.mean(token_temp * jnp.log(totals), axis=1)
    raised = jnp.exp(scores / list_temp) * count
    norm = lax.psum(jnp.sum(raised, axis=-1), "dp")
    score_grad = loss_scale * (raised / norm[:, None] - wanted) / list_temp
    token_grad = weights / totals[..., None] * (score_grad / QT)[:, None, :, None]
    token_narrow = token_grad.astype(jnp.bfloat16)
    doc_grad = (
        jnp.einsum("qiej,qid->ejd", token_narrow, every_query, preferred_element_type=jnp.float32)
        * inv_root
    )
    query_part = (
        jnp.einsum("qiej,ejd->qid", token_narrow, doc_narrow, preferred_element_type=jnp.float32)
        * inv_root
    )
    query_sum = lax.psum_scatter(query_part, "dp", scatter_dimension=0, tiled=True)
    proj_grad = doc_factor * (
        doc_grad - doc_unit * jnp.mean(doc_unit * doc_grad, axis=-1, keepdims=True)
    )
    proj_narrow = proj_grad.astype(jnp.bfloat16).reshape(enc_count * doc_tokens, EMB)
    grad_hidden = lax.dot_general(
        proj_narrow, proj_weight, (((1,), (1,)), ((), ())), preferred_element_type=jnp.float32
    ).astype(jnp.bfloat16)
    grad_hidden = grad_hidden.reshape(enc_count, doc_tokens, hidden_part)
    weight_part = lax.dot_general(
        flat_hidden, proj_narrow, (((0,), (0,)), ((), ())), preferred_element_type=jnp.float32
    )
    grad_weight = lax.psum(weight_part, "dp") / (enc_count * shards)
    grad_query = query_factor * (
        query_sum - query_unit * jnp.mean(query_unit * query_sum, axis=-1, keepdims=True)
    )
    return (grad_hidden, grad_weight, grad_query)


HIGH = lax.Precision.HIGHEST
MESH = pl.DeviceIdType.MESH


def grid_of(shape, dim):
    return lax.broadcasted_iota(jnp.int32, shape, dim)


def exchange_kernel(
    shards,
    enc_count,
    doc_tokens,
    hidden_hbm,
    weight_hbm,
    query_ref,
    list_ref,
    length_ref,
    narrow_ref,
    gathered_ref,
    query_grad_ref,
    hidden,
    weight,
    unit,
    factor,
    doc_narrow,
    weights,
    totals,
    token_narrow,
    narrow_t,
    queries,
    table_out,
    table_in,
    norms,
    part_out,
    part_in,
    pair_out,
    pair_in,
    chip_out,
    chip_in,
    own_sum,
    load_sem,
    query_send,
    query_recv,
    table_send,
    table_recv,
    norm_send,
    norm_recv,
    part_send,
    part_recv,
    pair_send,
    pair_recv,
    chip_send,
    chip_recv,
    ring_send,
    ring_recv,
    mate_send,
    mate_recv,
):
    f32, bf16 = jnp.float32, jnp.bfloat16
    me = lax.axis_index("dp")
    core = lax.rem(me, 2)
    chip = lax.div(me, 2)
    chips = shards // 2
    mate = chip * 2 + (1 - core)
    inv_root = 1.0 / math.sqrt(EMB)
    tokens, hid = hidden.shape
    lanes = shards * QT
    docs = 8
    block = docs * doc_tokens
    blocks = tokens // block
    chunk = hid // shards

    weight_copy = pltpu.make_async_copy(weight_hbm, weight, load_sem.at[blocks])
    weight_copy.start()

    def hidden_copy(b):
        rows = pl.ds(pl.multiple_of(b * block, block), block)
        return pltpu.make_async_copy(hidden_hbm.at[rows], hidden.at[rows], load_sem.at[b])

    for b in range(blocks):
        hidden_copy(b).start()

    barrier = pltpu.get_barrier_semaphore()
    for t in range(1, shards):
        pl.semaphore_signal(
            barrier, inc=1, device_id={"dp": lax.rem(me + t, shards)}, device_id_type=MESH
        )

    def remote(src, dst, send, recv, peer):
        return pltpu.make_async_remote_copy(
            src_ref=src,
            dst_ref=dst,
            send_sem=send,
            recv_sem=recv,
            device_id={"dp": peer},
            device_id_type=MESH,
        )

    query = query_ref[...].astype(f32)
    query_factor = lax.rsqrt(jnp.mean(query * query, axis=-1, keepdims=True) + epsilon)
    query_unit = query * query_factor
    queries[me] = query_unit.astype(bf16)
    slots = list_ref.shape[1]
    valid = list_ref[1:2, :]
    target = jnp.exp(list_ref[0:1, :]) * valid
    target = target / jnp.sum(target, axis=-1, keepdims=True)
    ident = list_ref[2:3, :]
    row = grid_of((8, slots), 0)
    terms = jnp.where(row == 0, valid, jnp.where(row == 1, target, 0.0))
    for p in range(shards):
        named = (grid_of((EMB, slots), 0) + p * EMB).astype(f32) == ident
        table_out[p] = lax.dot_general(
            terms,
            jnp.where(named, 1.0, 0.0),
            (((1,), (1,)), ((), ())),
            precision=HIGH,
            preferred_element_type=f32,
        )
    table_in[me] = table_out[me]

    pl.semaphore_wait(barrier, shards - 1)
    first = []
    for t in range(1, shards):
        peer = lax.rem(me + t, shards)
        first.append(
            remote(queries.at[me], queries.at[me], query_send.at[t], query_recv.at[t], peer)
        )
        first.append(
            remote(table_out.at[peer], table_in.at[me], table_send.at[t], table_recv.at[t], peer)
        )
    for copy in first:
        copy.start()

    weight_copy.wait()

    def project(b, carry):
        hidden_copy(b).wait()
        rows = pl.ds(pl.multiple_of(b * block, block), block)
        proj = jnp.dot(hidden[rows], weight[...], preferred_element_type=f32)
        scale = lax.rsqrt(jnp.mean(proj * proj, axis=-1, keepdims=True) + epsilon)
        values = proj * scale
        unit[rows] = values
        factor[rows] = jnp.broadcast_to(scale, values.shape)
        doc_narrow[rows] = values.astype(bf16)
        return carry

    lax.fori_loop(0, blocks, project, 0)

    for copy in first:
        copy.wait_recv()
    every = queries[...].reshape(lanes, EMB)

    def score(b, carry):
        rows = pl.ds(pl.multiple_of(b * block, block), block)
        some = pl.ds(pl.multiple_of(b * docs, docs), docs)
        product = lax.dot_general(
            doc_narrow[rows], every, (((1,), (1,)), ((), ())), preferred_element_type=f32
        )
        grown = jnp.exp(product * (inv_root / token_temp)).reshape(docs, doc_tokens, lanes)
        inside = grid_of((docs, doc_tokens, lanes), 1).astype(f32) < length_ref[some][:, None, :]
        grown = jnp.where(inside, grown, 0.0)
        weights[rows] = grown.reshape(block, lanes)
        totals[some] = jnp.sum(grown, axis=1)
        return carry

    lax.fori_loop(0, blocks, score, 0)

    table = table_in[...].reshape(shards * 8, EMB)
    place = grid_of((shards * 8, lanes), 0)
    wanted_place = lax.div(grid_of((shards * 8, lanes), 1), QT) * 8

    def spread(r):
        return lax.dot_general(
            table,
            jnp.where(place == wanted_place + r, 1.0, 0.0),
            (((0,), (0,)), ((), ())),
            precision=HIGH,
            preferred_element_type=f32,
        )[:enc_count]

    count = spread(0)
    wanted = spread(1)
    total = totals[...]
    same = lax.div(grid_of((lanes, lanes), 0), QT) == lax.div(grid_of((lanes, lanes), 1), QT)
    scores = jnp.dot(
        jnp.log(total),
        jnp.where(same, token_temp / QT, 0.0),
        precision=HIGH,
        preferred_element_type=f32,
    )
    raised = jnp.exp(scores / list_temp) * count
    gather = jnp.where(grid_of((lanes, EMB), 0) == grid_of((lanes, EMB), 1) * QT, 1.0, 0.0)
    norms[me] = jnp.dot(
        jnp.broadcast_to(jnp.sum(raised, axis=0, keepdims=True), (8, lanes)),
        gather,
        precision=HIGH,
        preferred_element_type=f32,
    )
    second = []
    for t in range(1, shards):
        peer = lax.rem(me + t, shards)
        second.append(remote(norms.at[me], norms.at[me], norm_send.at[t], norm_recv.at[t], peer))
    for copy in second:
        copy.start()
    for copy in second:
        copy.wait_recv()
    back = jnp.where(grid_of((EMB, lanes), 0) == lax.div(grid_of((EMB, lanes), 1), QT), 1.0, 0.0)
    norm = jnp.dot(
        jnp.sum(norms[...], axis=0), back, precision=HIGH, preferred_element_type=f32
    )[0:1]
    score_grad = loss_scale * (raised / norm - wanted) / list_temp
    totals[...] = (score_grad / QT) / total

    def backward(b, carry):
        rows = pl.ds(pl.multiple_of(b * block, block), block)
        some = pl.ds(pl.multiple_of(b * docs, docs), docs)
        grads = weights[rows].reshape(docs, doc_tokens, lanes) * totals[some][:, None, :]
        narrow = grads.reshape(block, lanes).astype(bf16)
        token_narrow[rows] = narrow
        doc_grad = jnp.dot(narrow, every, preferred_element_type=f32) * inv_root
        values = unit[rows]
        proj_grad = factor[rows] * (
            doc_grad - values * jnp.mean(values * doc_grad, axis=-1, keepdims=True)
        )
        narrow_ref[rows] = proj_grad.astype(bf16)
        narrow_t[b] = jnp.transpose(proj_grad).astype(bf16)
        return carry

    lax.fori_loop(0, blocks, backward, 0)

    def weight_part(c):
        columns = pl.ds(pl.multiple_of(c * chunk, chunk), chunk)
        total = jnp.zeros((EMB, chunk), f32)
        for b in range(blocks):
            total = total + jnp.dot(
                narrow_t[b], hidden[b * block : (b + 1) * block, columns],
                preferred_element_type=f32,
            )
        return total

    pairs = [
        remote(pair_out.at[t], pair_in.at[t], pair_send.at[t], pair_recv.at[t], mate)
        for t in range(chips)
    ]
    across = []
    for t in range(chips + 1):
        if t < chips:
            there = lax.rem(chip + 1 + t, chips)
            pair_out[t] = weight_part(there * 2 + (1 - core)).astype(bf16)
            pairs[t].start()
        if t > 0:
            s = t - 1
            there = lax.rem(chip + 1 + s, chips)
            part = weight_part(there * 2 + core)
            pairs[s].wait_recv()
            part = part + pair_in[s].astype(f32)
            if s < chips - 1:
                chip_out[s] = part.astype(bf16)
                copy = remote(
                    chip_out.at[s],
                    chip_in.at[s],
                    chip_send.at[s],
                    chip_recv.at[s],
                    there * 2 + core,
                )
                copy.start()
                across.append(copy)
            else:
                own_sum[...] = part

    def query_part(b, sums):
        rows = pl.ds(pl.multiple_of(b * block, block), block)
        return sums + lax.dot_general(
            token_narrow[rows],
            doc_narrow[rows],
            (((0,), (0,)), ((), ())),
            preferred_element_type=f32,
        )

    sums = lax.fori_loop(0, blocks, query_part, jnp.zeros((lanes, EMB), f32))
    part_out[...] = sums.reshape(shards, QT, EMB)
    third = []
    for t in range(1, shards):
        peer = lax.rem(me + t, shards)
        third.append(
            remote(part_out.at[peer], part_in.at[t], part_send.at[t], part_recv.at[t], peer)
        )
    for copy in third:
        copy.start()

    for copy in across:
        copy.wait_recv()
    reduced = own_sum[...]
    for s in range(chips - 1):
        reduced = reduced + chip_in[s].astype(f32)
    own_rows = pl.ds(pl.multiple_of(me * chunk, chunk), chunk)
    gathered_ref[own_rows] = jnp.transpose(reduced * (1.0 / (enc_count * shards))).astype(bf16)

    ring = []
    for s in range(chips - 1):
        there = lax.rem(chip + 1 + s, chips)
        ring.append(
            remote(
                gathered_ref.at[own_rows],
                gathered_ref.at[own_rows],
                ring_send.at[s],
                ring_recv.at[s],
                there * 2 + core,
            )
        )
    for copy in ring:
        copy.start()
    to_mate = [
        remote(
            gathered_ref.at[own_rows],
            gathered_ref.at[own_rows],
            mate_send.at[chips - 1],
            mate_recv.at[chips - 1],
            mate,
        )
    ]
    to_mate[0].start()

    for copy in third:
        copy.wait_recv()
    query_sum = part_out[me]
    for t in range(1, shards):
        query_sum = query_sum + part_in[t]
    query_sum = query_sum * inv_root
    query_grad_ref[...] = query_factor * (
        query_sum - query_unit * jnp.mean(query_unit * query_sum, axis=-1, keepdims=True)
    )

    for s in range(chips - 1):
        ring[s].wait_recv()
        source = lax.rem(chip + 2 * chips - 1 - s, chips) * 2 + core
        rows = pl.ds(pl.multiple_of(source * chunk, chunk), chunk)
        copy = remote(
            gathered_ref.at[rows], gathered_ref.at[rows], mate_send.at[s], mate_recv.at[s], mate
        )
        copy.start()
        to_mate.append(copy)
    for copy in to_mate:
        copy.wait_recv()
    for copy in first + second + third + pairs + across + ring + to_mate:
        copy.wait_send()


def exchange(flat_hidden, proj_weight, query, lists, lengths, shards, enc_count, doc_tokens):
    tokens, hid = flat_hidden.shape
    lanes = shards * QT
    docs = 8
    block = docs * doc_tokens
    blocks = tokens // block
    chunk = hid // shards
    chips = shards // 2
    f32, bf16 = jnp.float32, jnp.bfloat16
    in_vmem = pl.BlockSpec(memory_space=pltpu.VMEM)
    in_hbm = pl.BlockSpec(memory_space=pl.ANY)
    dma = pltpu.SemaphoreType.DMA
    return pl.pallas_call(
        functools.partial(exchange_kernel, shards, enc_count, doc_tokens),
        out_shape=(
            jax.ShapeDtypeStruct((tokens, EMB), bf16),
            jax.ShapeDtypeStruct((hid, EMB), bf16),
            jax.ShapeDtypeStruct((QT, EMB), f32),
        ),
        in_specs=[in_hbm, in_hbm, in_vmem, in_vmem, in_vmem],
        out_specs=(in_vmem, in_vmem, in_vmem),
        scratch_shapes=[
            pltpu.VMEM((tokens, hid), bf16),
            pltpu.VMEM((hid, EMB), bf16),
            pltpu.VMEM((tokens, EMB), f32),
            pltpu.VMEM((tokens, EMB), f32),
            pltpu.VMEM((tokens, EMB), bf16),
            pltpu.VMEM((tokens, lanes), f32),
            pltpu.VMEM((enc_count, lanes), f32),
            pltpu.VMEM((tokens, lanes), bf16),
            pltpu.VMEM((blocks, EMB, block), bf16),
            pltpu.VMEM((shards, QT, EMB), bf16),
            pltpu.VMEM((shards, 8, EMB), f32),
            pltpu.VMEM((shards, 8, EMB), f32),
            pltpu.VMEM((shards, 8, EMB), f32),
            pltpu.VMEM((shards, QT, EMB), f32),
            pltpu.VMEM((shards, QT, EMB), f32),
            pltpu.VMEM((chips, EMB, chunk), bf16),
            pltpu.VMEM((chips, EMB, chunk), bf16),
            pltpu.VMEM((chips, EMB, chunk), bf16),
            pltpu.VMEM((chips, EMB, chunk), bf16),
            pltpu.VMEM((EMB, chunk), f32),
            dma((blocks + 1,)),
        ]
        + [dma((shards,))] * 8
        + [dma((chips,))] * 8,
        compiler_params=pltpu.CompilerParams(
            collective_id=0, has_side_effects=True, vmem_limit_bytes=48 * 1024 * 1024
        ),
    )(flat_hidden, proj_weight, query, lists, lengths)


def spread_kernel(narrow_ref, weight_ref, gathered_ref, hidden_grad_ref, weight_grad_ref):
    hidden_grad_ref[...] = lax.dot_general(
        narrow_ref[...],
        weight_ref[...],
        (((1,), (1,)), ((), ())),
        preferred_element_type=jnp.float32,
    ).astype(jnp.bfloat16)
    weight_grad_ref[...] = gathered_ref[...].astype(jnp.float32)


def hidden_gradient(proj_narrow, proj_weight, gathered, steps=8):
    tokens = proj_narrow.shape[0]
    hid = proj_weight.shape[0]
    return pl.pallas_call(
        spread_kernel,
        grid=(steps,),
        out_shape=(
            jax.ShapeDtypeStruct((tokens, hid), jnp.bfloat16),
            jax.ShapeDtypeStruct((hid, EMB), jnp.float32),
        ),
        in_specs=[
            pl.BlockSpec((tokens // steps, EMB), lambda i: (i, 0)),
            pl.BlockSpec((hid, EMB), lambda i: (0, 0)),
            pl.BlockSpec((hid // steps, EMB), lambda i: (i, 0)),
        ],
        out_specs=(
            pl.BlockSpec((tokens // steps, hid), lambda i: (i, 0)),
            pl.BlockSpec((hid // steps, EMB), lambda i: (i, 0)),
        ),
        compiler_params=pltpu.CompilerParams(vmem_limit_bytes=48 * 1024 * 1024),
    )(proj_narrow, proj_weight, gathered)


def with_kernels(
    doc_hidden, proj_weight, query_reps, teacher, cand_peer, cand_doc, tile_count, doc_len
):
    enc_count, doc_tokens, hidden_part = doc_hidden.shape
    shards = lax.axis_size("dp")
    me = lax.axis_index("dp")
    slots = cand_doc.shape[1]
    valid = (jnp.arange(slots)[None, :] // TILE < tile_count[:, None]).astype(jnp.float32)
    ident = (cand_peer[:, :, 0] * EMB + cand_doc).astype(jnp.float32)
    lists = jnp.concatenate(
        [teacher, valid, ident, jnp.zeros((5, slots), jnp.float32)], axis=0
    )
    own_len = lax.dynamic_slice_in_dim(doc_len, me * enc_count, enc_count).astype(jnp.float32)
    lengths = jnp.broadcast_to(own_len[:, None], (enc_count, shards * QT))
    proj_narrow, gathered, grad_query = exchange(
        doc_hidden.reshape(enc_count * doc_tokens, hidden_part),
        proj_weight,
        query_reps.reshape(QT, EMB),
        lists,
        lengths,
        shards,
        enc_count,
        doc_tokens,
    )
    grad_hidden, grad_weight = hidden_gradient(proj_narrow, proj_weight, gathered)
    return (
        grad_hidden.reshape(enc_count, doc_tokens, hidden_part),
        grad_weight,
        grad_query.reshape(1, QT, EMB),
    )


def solution(mesh):
    plain = mesh.shape["tensor"] > 1 or mesh.shape["dp"] % 2 > 0
    placed = (
        P(("groups", "dp"), None, "tensor"),
        P("tensor", None),
        P(("groups", "dp"), None, None),
        P(("groups", "dp"), None),
        P(("groups", "dp"), None, None),
        P(("groups", "dp"), None),
        P(("groups", "dp")),
        P("groups"),
    )
    return jax.shard_map(
        with_collectives if plain else with_kernels,
        mesh=mesh,
        in_specs=placed,
        out_specs=(
            P(("groups", "dp"), None, "tensor"),
            P(("groups", "tensor"), None),
            P(("groups", "dp"), None, None),
        ),
        check_vma=False,
    )
```

```python
import functools
import math

import jax
import jax.numpy as jnp
from jax import lax
from jax.experimental import pallas as pl
from jax.experimental.pallas import tpu as pltpu
from jax.sharding import PartitionSpec as P

EMB = 128
QT = 32
TILE = 128

token_temp = 0.5
list_temp = 0.2
loss_scale = 4096.0
epsilon = 1e-06


def unit_rows(values):
    factor = lax.rsqrt(jnp.mean(values * values, axis=-1, keepdims=True) + epsilon)
    return (values * factor, factor)


def list_tables(teacher, cand_peer, cand_doc, tile_count, shards, enc_count):
    slot_count = cand_doc.shape[1]
    valid = (jnp.arange(slot_count)[None, :] // TILE < tile_count[:, None]).astype(jnp.float32)
    target = jnp.exp(teacher) * valid
    target = target / jnp.sum(target, axis=-1, keepdims=True)
    ident = cand_peer[:, :, 0] * enc_count + cand_doc
    named = ident[:, :, None] == jnp.arange(shards * enc_count, dtype=jnp.int32)[None, None, :]
    count = jnp.sum(jnp.where(named, valid[:, :, None], 0.0), axis=1)
    wanted = jnp.sum(jnp.where(named, target[:, :, None], 0.0), axis=1)
    return count, wanted


def with_collectives(
    doc_hidden, proj_weight, query_reps, teacher, cand_peer, cand_doc, tile_count, doc_len
):
    enc_count, doc_tokens, hidden_part = doc_hidden.shape
    shards = lax.axis_size("dp")
    me = lax.axis_index("dp")
    inv_root = 1.0 / math.sqrt(EMB)
    query_unit, query_factor = unit_rows(query_reps.astype(jnp.float32))
    query_narrow = query_unit.astype(jnp.bfloat16)
    count, wanted = list_tables(teacher, cand_peer, cand_doc, tile_count, shards, enc_count)
    every_query = lax.all_gather(query_narrow, "dp", axis=0, tiled=True)
    tables = lax.all_gather(jnp.stack([count, wanted], axis=1), "dp", axis=0, tiled=True)
    tables = lax.dynamic_slice_in_dim(tables, me * enc_count, enc_count, axis=2)
    count, wanted = tables[:, 0], tables[:, 1]
    flat_hidden = doc_hidden.reshape(enc_count * doc_tokens, hidden_part)
    proj_part = jnp.dot(flat_hidden, proj_weight, preferred_element_type=jnp.float32)
    doc_proj = lax.psum(proj_part, "tensor").reshape(enc_count, doc_tokens, EMB)
    doc_unit, doc_factor = unit_rows(doc_proj)
    doc_narrow = doc_unit.astype(jnp.bfloat16)
    own_len = lax.dynamic_slice_in_dim(doc_len, me * enc_count, enc_count)
    token_mask = (jnp.arange(doc_tokens)[None, :] < own_len[:, None]).astype(jnp.float32)
    similarity = (
        jnp.einsum("qid,ejd->qiej", every_query, doc_narrow, preferred_element_type=jnp.float32)
        * inv_root
    )
    weights = jnp.exp(similarity / token_temp) * token_mask
    totals = jnp.sum(weights, axis=-1)
    scores = jnp.mean(token_temp * jnp.log(totals), axis=1)
    raised = jnp.exp(scores / list_temp) * count
    norm = lax.psum(jnp.sum(raised, axis=-1), "dp")
    score_grad = loss_scale * (raised / norm[:, None] - wanted) / list_temp
    token_grad = weights / totals[..., None] * (score_grad / QT)[:, None, :, None]
    token_narrow = token_grad.astype(jnp.bfloat16)
    doc_grad = (
        jnp.einsum("qiej,qid->ejd", token_narrow, every_query, preferred_element_type=jnp.float32)
        * inv_root
    )
    query_part = (
        jnp.einsum("qiej,ejd->qid", token_narrow, doc_narrow, preferred_element_type=jnp.float32)
        * inv_root
    )
    query_sum = lax.psum_scatter(query_part, "dp", scatter_dimension=0, tiled=True)
    proj_grad = doc_factor * (
        doc_grad - doc_unit * jnp.mean(doc_unit * doc_grad, axis=-1, keepdims=True)
    )
    proj_narrow = proj_grad.astype(jnp.bfloat16).reshape(enc_count * doc_tokens, EMB)
    grad_hidden = lax.dot_general(
        proj_narrow, proj_weight, (((1,), (1,)), ((), ())), preferred_element_type=jnp.float32
    ).astype(jnp.bfloat16)
    grad_hidden = grad_hidden.reshape(enc_count, doc_tokens, hidden_part)
    weight_part = lax.dot_general(
        flat_hidden, proj_narrow, (((0,), (0,)), ((), ())), preferred_element_type=jnp.float32
    )
    grad_weight = lax.psum(weight_part, "dp") / (enc_count * shards)
    grad_query = query_factor * (
        query_sum - query_unit * jnp.mean(query_unit * query_sum, axis=-1, keepdims=True)
    )
    return (grad_hidden, grad_weight, grad_query)


HIGH = lax.Precision.HIGHEST
MESH = pl.DeviceIdType.MESH


def grid_of(shape, dim):
    return lax.broadcasted_iota(jnp.int32, shape, dim)


def exchange_kernel(
    shards,
    enc_count,
    doc_tokens,
    hidden_hbm,
    weight_hbm,
    query_ref,
    list_ref,
    length_ref,
    narrow_ref,
    gathered_ref,
    query_grad_ref,
    weight_t_ref,
    hidden,
    weight,
    unit,
    factor,
    doc_narrow,
    weights,
    totals,
    token_narrow,
    narrow_t,
    queries,
    table_out,
    table_in,
    norms,
    part_out,
    part_in,
    pair_out,
    pair_in,
    chip_out,
    chip_in,
    side_out,
    side_in,
    own_sum,
    load_sem,
    query_send,
    query_recv,
    table_send,
    table_recv,
    norm_send,
    norm_recv,
    part_send,
    part_recv,
    pair_send,
    pair_recv,
    chip_send,
    chip_recv,
    ring_send,
    ring_recv,
    mate_send,
    mate_recv,
    side_send,
    side_recv,
    fan_send,
    fan_recv,
):
    f32, bf16 = jnp.float32, jnp.bfloat16
    me = lax.axis_index("dp")
    core = lax.rem(me, 2)
    chip = lax.div(me, 2)
    chips = shards // 2
    mate = chip * 2 + (1 - core)
    lines = chips // 2
    line, side = lax.div(chip, 2), lax.rem(chip, 2)
    beside = (line * 2 + 1 - side) * 2 + core

    def shard_at(line_at, side_at, core_at):
        return (line_at * 2 + side_at) * 2 + core_at

    inv_root = 1.0 / math.sqrt(EMB)
    tokens, hid = hidden.shape
    lanes = shards * QT
    docs = 8
    block = docs * doc_tokens
    blocks = tokens // block
    chunk = hid // shards

    weight_copy = pltpu.make_async_copy(weight_hbm, weight, load_sem.at[blocks])
    weight_copy.start()

    def hidden_copy(b):
        rows = pl.ds(pl.multiple_of(b * block, block), block)
        return pltpu.make_async_copy(hidden_hbm.at[rows], hidden.at[rows], load_sem.at[b])

    for b in range(blocks):
        hidden_copy(b).start()

    barrier = pltpu.get_barrier_semaphore()
    for t in range(1, shards):
        pl.semaphore_signal(
            barrier, inc=1, device_id={"dp": lax.rem(me + t, shards)}, device_id_type=MESH
        )

    def remote(src, dst, send, recv, peer):
        return pltpu.make_async_remote_copy(
            src_ref=src,
            dst_ref=dst,
            send_sem=send,
            recv_sem=recv,
            device_id={"dp": peer},
            device_id_type=MESH,
        )

    query = query_ref[...].astype(f32)
    query_factor = lax.rsqrt(jnp.mean(query * query, axis=-1, keepdims=True) + epsilon)
    query_unit = query * query_factor
    queries[me] = query_unit.astype(bf16)
    slots = list_ref.shape[1]
    valid = list_ref[1:2, :]
    target = jnp.exp(list_ref[0:1, :]) * valid
    target = target / jnp.sum(target, axis=-1, keepdims=True)
    ident = list_ref[2:3, :]
    row = grid_of((8, slots), 0)
    high = target.astype(bf16).astype(f32)
    middle = (target - high).astype(bf16).astype(f32)
    low = target - high - middle
    terms = jnp.where(
        row == 0,
        valid,
        jnp.where(
            row == 1, high, jnp.where(row == 2, middle, jnp.where(row == 3, low, 0.0))
        ),
    ).astype(bf16)
    for p in range(shards):
        named = (grid_of((EMB, slots), 0) + p * EMB).astype(f32) == ident
        table_out[p] = lax.dot_general(
            terms,
            jnp.where(named, 1.0, 0.0).astype(bf16),
            (((1,), (1,)), ((), ())),
            preferred_element_type=f32,
        )
    table_in[me] = table_out[me]

    pl.semaphore_wait(barrier, shards - 1)
    first = []
    for t in range(1, shards):
        peer = lax.rem(me + t, shards)
        first.append(
            remote(queries.at[me], queries.at[me], query_send.at[t], query_recv.at[t], peer)
        )
        first.append(
            remote(table_out.at[peer], table_in.at[me], table_send.at[t], table_recv.at[t], peer)
        )
    for copy in first:
        copy.start()

    weight_copy.wait()

    def project(b, carry):
        hidden_copy(b).wait()
        rows = pl.ds(pl.multiple_of(b * block, block), block)
        proj = jnp.dot(hidden[rows], weight[...], preferred_element_type=f32)
        scale = lax.rsqrt(jnp.mean(proj * proj, axis=-1, keepdims=True) + epsilon)
        values = proj * scale
        unit[rows] = values
        factor[rows] = jnp.broadcast_to(scale, values.shape)
        doc_narrow[rows] = values.astype(bf16)
        return carry

    lax.fori_loop(0, blocks, project, 0)

    for copy in first:
        copy.wait_recv()
    every = queries[...].reshape(lanes, EMB)

    def score(b, carry):
        rows = pl.ds(pl.multiple_of(b * block, block), block)
        some = pl.ds(pl.multiple_of(b * docs, docs), docs)
        product = lax.dot_general(
            doc_narrow[rows], every, (((1,), (1,)), ((), ())), preferred_element_type=f32
        )
        grown = jnp.exp(product * (inv_root / token_temp)).reshape(docs, doc_tokens, lanes)
        inside = grid_of((docs, doc_tokens, lanes), 1).astype(f32) < length_ref[some][:, None, :]
        grown = jnp.where(inside, grown, 0.0)
        weights[rows] = grown.reshape(block, lanes)
        totals[some] = jnp.sum(grown, axis=1)
        return carry

    lax.fori_loop(0, blocks, score, 0)

    table = table_in[...].reshape(shards * 8, EMB)
    place = grid_of((shards * 8, lanes), 0)
    wanted_place = lax.div(grid_of((shards * 8, lanes), 1), QT) * 8

    def spread(r, last):
        return lax.dot_general(
            table,
            jnp.where((place >= wanted_place + r) & (place <= wanted_place + last), 1.0, 0.0),
            (((0,), (0,)), ((), ())),
            precision=HIGH,
            preferred_element_type=f32,
        )[:enc_count]

    count = spread(0, 0)
    wanted = spread(1, 3)
    total = totals[...]
    same = lax.div(grid_of((lanes, lanes), 0), QT) == lax.div(grid_of((lanes, lanes), 1), QT)
    scores = jnp.dot(
        jnp.log(total),
        jnp.where(same, token_temp / QT, 0.0),
        precision=HIGH,
        preferred_element_type=f32,
    )
    raised = jnp.exp(scores / list_temp) * count
    gather = jnp.where(grid_of((lanes, EMB), 0) == grid_of((lanes, EMB), 1) * QT, 1.0, 0.0)
    norms[me] = jnp.dot(
        jnp.broadcast_to(jnp.sum(raised, axis=0, keepdims=True), (8, lanes)),
        gather,
        precision=HIGH,
        preferred_element_type=f32,
    )
    second = []
    for t in range(1, shards):
        peer = lax.rem(me + t, shards)
        second.append(remote(norms.at[me], norms.at[me], norm_send.at[t], norm_recv.at[t], peer))
    for copy in second:
        copy.start()
    for copy in second:
        copy.wait_recv()
    back = jnp.where(grid_of((EMB, lanes), 0) == lax.div(grid_of((EMB, lanes), 1), QT), 1.0, 0.0)
    norm = jnp.dot(
        jnp.sum(norms[...], axis=0), back, precision=HIGH, preferred_element_type=f32
    )[0:1]
    score_grad = loss_scale * (raised / norm - wanted) / list_temp
    totals[...] = (score_grad / QT) / total

    def backward(b, carry):
        rows = pl.ds(pl.multiple_of(b * block, block), block)
        some = pl.ds(pl.multiple_of(b * docs, docs), docs)
        grads = weights[rows].reshape(docs, doc_tokens, lanes) * totals[some][:, None, :]
        narrow = grads.reshape(block, lanes).astype(bf16)
        token_narrow[rows] = narrow
        doc_grad = jnp.dot(narrow, every, preferred_element_type=f32) * inv_root
        values = unit[rows]
        proj_grad = factor[rows] * (
            doc_grad - values * jnp.mean(values * doc_grad, axis=-1, keepdims=True)
        )
        narrow_ref[rows] = proj_grad.astype(bf16)
        narrow_t[b] = jnp.transpose(proj_grad).astype(bf16)
        return carry

    lax.fori_loop(0, blocks, backward, 0)

    def weight_part(c):
        columns = pl.ds(pl.multiple_of(c * chunk, chunk), chunk)
        total = jnp.zeros((EMB, chunk), f32)
        for b in range(blocks):
            total = total + jnp.dot(
                narrow_t[b], hidden[b * block : (b + 1) * block, columns],
                preferred_element_type=f32,
            )
        return total

    pairs = [
        remote(pair_out.at[t], pair_in.at[t], pair_send.at[t], pair_recv.at[t], mate)
        for t in range(chips)
    ]
    across = []
    sides = [
        remote(side_out.at[t], side_in.at[t], side_send.at[t], side_recv.at[t], beside)
        for t in range(lines)
    ]

    def bound_for(t):
        there = lax.rem(line + 1 + t % lines, lines)
        return there, (1 - side if t < lines else side)

    for t in range(chips + 1):
        if t < chips:
            there, at = bound_for(t)
            pair_out[t] = weight_part(shard_at(there, at, 1 - core)).astype(bf16)
            pairs[t].start()
        if t > 0:
            s = t - 1
            there, at = bound_for(s)
            part = weight_part(shard_at(there, at, core))
            pairs[s].wait_recv()
            part = part + pair_in[s].astype(f32)
            if s < lines:
                side_out[s] = part.astype(bf16)
                sides[s].start()
            else:
                k = s - lines
                sides[k].wait_recv()
                part = part + side_in[k].astype(f32)
                if k < lines - 1:
                    chip_out[k] = part.astype(bf16)
                    copy = remote(
                        chip_out.at[k],
                        chip_in.at[k],
                        chip_send.at[k],
                        chip_recv.at[k],
                        shard_at(there, side, core),
                    )
                    copy.start()
                    across.append(copy)
                else:
                    own_sum[...] = part

    def query_part(b, sums):
        rows = pl.ds(pl.multiple_of(b * block, block), block)
        return sums + lax.dot_general(
            token_narrow[rows],
            doc_narrow[rows],
            (((0,), (0,)), ((), ())),
            preferred_element_type=f32,
        )

    sums = lax.fori_loop(0, blocks, query_part, jnp.zeros((lanes, EMB), f32))
    part_out[...] = sums.reshape(shards, QT, EMB)
    third = []
    for t in range(1, shards):
        peer = lax.rem(me + t, shards)
        third.append(
            remote(part_out.at[peer], part_in.at[t], part_send.at[t], part_recv.at[t], peer)
        )
    for copy in third:
        copy.start()

    for p in range(shards):
        weight_t_ref[:, p * chunk : (p + 1) * chunk] = jnp.transpose(
            weight[p * chunk : (p + 1) * chunk]
        )

    for copy in across:
        copy.wait_recv()
    reduced = own_sum[...]
    for s in range(lines - 1):
        reduced = reduced + chip_in[s].astype(f32)
    own_rows = pl.ds(pl.multiple_of(me * chunk, chunk), chunk)
    gathered_ref[own_rows] = jnp.transpose(reduced * (1.0 / (enc_count * shards))).astype(bf16)

    def pass_on(source, send, recv, peer):
        rows = pl.ds(pl.multiple_of(source * chunk, chunk), chunk)
        copy = remote(gathered_ref.at[rows], gathered_ref.at[rows], send, recv, peer)
        copy.start()
        return copy

    ring = []
    for s in range(lines - 1):
        there = lax.rem(line + 1 + s, lines)
        ring.append(
            pass_on(me, ring_send.at[s], ring_recv.at[s], shard_at(there, side, core))
        )
    fan = [pass_on(me, fan_send.at[lines - 1], fan_recv.at[lines - 1], beside)]
    to_mate = [pass_on(me, mate_send.at[lines - 1], mate_recv.at[lines - 1], mate)]

    for copy in third:
        copy.wait_recv()
    query_sum = part_out[me]
    for t in range(1, shards):
        query_sum = query_sum + part_in[t]
    query_sum = query_sum * inv_root
    query_grad_ref[...] = query_factor * (
        query_sum - query_unit * jnp.mean(query_unit * query_sum, axis=-1, keepdims=True)
    )

    def from_beside(slot, line_at):
        fan[0 if slot == lines - 1 else slot + 1].wait_recv()
        to_mate.append(
            pass_on(
                shard_at(line_at, 1 - side, core),
                mate_send.at[lines + slot],
                mate_recv.at[lines + slot],
                mate,
            )
        )

    from_beside(lines - 1, line)
    sources = [lax.rem(line + 2 * lines - 1 - s, lines) for s in range(lines - 1)]
    for s in range(lines - 1):
        ring[s].wait_recv()
        source = shard_at(sources[s], side, core)
        fan.append(pass_on(source, fan_send.at[s], fan_recv.at[s], beside))
        to_mate.append(pass_on(source, mate_send.at[s], mate_recv.at[s], mate))
    for s in range(lines - 1):
        from_beside(s, sources[s])
    for copy in to_mate:
        copy.wait_recv()
    for copy in first + second + third + pairs + sides + across + ring + fan + to_mate:
        copy.wait_send()


def exchange(flat_hidden, proj_weight, query, lists, lengths, shards, enc_count, doc_tokens):
    tokens, hid = flat_hidden.shape
    lanes = shards * QT
    docs = 8
    block = docs * doc_tokens
    blocks = tokens // block
    chunk = hid // shards
    chips = shards // 2
    f32, bf16 = jnp.float32, jnp.bfloat16
    in_vmem = pl.BlockSpec(memory_space=pltpu.VMEM)
    in_hbm = pl.BlockSpec(memory_space=pltpu.HBM)
    dma = pltpu.SemaphoreType.DMA
    return pl.pallas_call(
        functools.partial(exchange_kernel, shards, enc_count, doc_tokens),
        out_shape=(
            jax.ShapeDtypeStruct((tokens, EMB), bf16),
            jax.ShapeDtypeStruct((hid, EMB), bf16),
            jax.ShapeDtypeStruct((QT, EMB), f32),
            jax.ShapeDtypeStruct((EMB, hid), bf16),
        ),
        in_specs=[in_hbm, in_hbm, in_vmem, in_vmem, in_vmem],
        out_specs=(in_vmem, in_vmem, in_vmem, in_vmem),
        scratch_shapes=[
            pltpu.VMEM((tokens, hid), bf16),
            pltpu.VMEM((hid, EMB), bf16),
            pltpu.VMEM((tokens, EMB), f32),
            pltpu.VMEM((tokens, EMB), f32),
            pltpu.VMEM((tokens, EMB), bf16),
            pltpu.VMEM((tokens, lanes), f32),
            pltpu.VMEM((enc_count, lanes), f32),
            pltpu.VMEM((tokens, lanes), bf16),
            pltpu.VMEM((blocks, EMB, block), bf16),
            pltpu.VMEM((shards, QT, EMB), bf16),
            pltpu.VMEM((shards, 8, EMB), f32),
            pltpu.VMEM((shards, 8, EMB), f32),
            pltpu.VMEM((shards, 8, EMB), f32),
            pltpu.VMEM((shards, QT, EMB), f32),
            pltpu.VMEM((shards, QT, EMB), f32),
            pltpu.VMEM((chips, EMB, chunk), bf16),
            pltpu.VMEM((chips, EMB, chunk), bf16),
            pltpu.VMEM((chips, EMB, chunk), bf16),
            pltpu.VMEM((chips, EMB, chunk), bf16),
            pltpu.VMEM((chips // 2, EMB, chunk), bf16),
            pltpu.VMEM((chips // 2, EMB, chunk), bf16),
            pltpu.VMEM((EMB, chunk), f32),
            dma((blocks + 1,)),
        ]
        + [dma((shards,))] * 8
        + [dma((chips,))] * 12,
        compiler_params=pltpu.CompilerParams(
            collective_id=0, has_side_effects=True, vmem_limit_bytes=48 * 1024 * 1024
        ),
    )(flat_hidden, proj_weight, query, lists, lengths)


def spread_kernel(narrow_ref, weight_t_ref, gathered_ref, hidden_grad_ref, weight_grad_ref):
    hidden_grad_ref[...] = jnp.dot(
        narrow_ref[...], weight_t_ref[...], preferred_element_type=jnp.float32
    ).astype(jnp.bfloat16)
    weight_grad_ref[...] = gathered_ref[...].astype(jnp.float32)


def hidden_gradient(proj_narrow, weight_t, gathered, steps=8):
    tokens = proj_narrow.shape[0]
    hid = weight_t.shape[1]
    return pl.pallas_call(
        spread_kernel,
        grid=(steps,),
        out_shape=(
            jax.ShapeDtypeStruct((tokens, hid), jnp.bfloat16),
            jax.ShapeDtypeStruct((hid, EMB), jnp.float32),
        ),
        in_specs=[
            pl.BlockSpec((tokens // steps, EMB), lambda i: (i, 0)),
            pl.BlockSpec((EMB, hid), lambda i: (0, 0)),
            pl.BlockSpec((hid // steps, EMB), lambda i: (i, 0)),
        ],
        out_specs=(
            pl.BlockSpec((tokens // steps, hid), lambda i: (i, 0)),
            pl.BlockSpec((hid // steps, EMB), lambda i: (i, 0)),
        ),
        compiler_params=pltpu.CompilerParams(vmem_limit_bytes=48 * 1024 * 1024),
    )(proj_narrow, weight_t, gathered)


def with_kernels(
    doc_hidden, proj_weight, query_reps, teacher, cand_peer, cand_doc, tile_count, doc_len
):
    enc_count, doc_tokens, hidden_part = doc_hidden.shape
    shards = lax.axis_size("dp")
    me = lax.axis_index("dp")
    slots = cand_doc.shape[1]
    valid = (jnp.arange(slots)[None, :] // TILE < tile_count[:, None]).astype(jnp.float32)
    ident = (cand_peer[:, :, 0] * EMB + cand_doc).astype(jnp.float32)
    lists = jnp.concatenate(
        [teacher, valid, ident, jnp.zeros((5, slots), jnp.float32)], axis=0
    )
    own_len = lax.dynamic_slice_in_dim(doc_len, me * enc_count, enc_count).astype(jnp.float32)
    lengths = jnp.broadcast_to(own_len[:, None], (enc_count, shards * QT))
    proj_narrow, gathered, grad_query, weight_t = exchange(
        doc_hidden.reshape(enc_count * doc_tokens, hidden_part),
        proj_weight,
        query_reps.reshape(QT, EMB),
        lists,
        lengths,
        shards,
        enc_count,
        doc_tokens,
    )
    grad_hidden, grad_weight = hidden_gradient(proj_narrow, weight_t, gathered)
    return (
        grad_hidden.reshape(enc_count, doc_tokens, hidden_part),
        grad_weight,
        grad_query.reshape(1, QT, EMB),
    )


def solution(mesh):
    plain = mesh.shape["tensor"] > 1 or mesh.shape["dp"] % 4 > 0
    placed = (
        P(("groups", "dp"), None, "tensor"),
        P("tensor", None),
        P(("groups", "dp"), None, None),
        P(("groups", "dp"), None),
        P(("groups", "dp"), None, None),
        P(("groups", "dp"), None),
        P(("groups", "dp")),
        P("groups"),
    )
    return jax.shard_map(
        with_collectives if plain else with_kernels,
        mesh=mesh,
        in_specs=placed,
        out_specs=(
            P(("groups", "dp"), None, "tensor"),
            P(("groups", "tensor"), None),
            P(("groups", "dp"), None, None),
        ),
        check_vma=False,
    )
```

```python
import functools
import math

import jax
import jax.numpy as jnp
from jax import lax
from jax.experimental import pallas as pl
from jax.experimental.pallas import tpu as pltpu
from jax.sharding import PartitionSpec as P

EMB = 128
QT = 32
TILE = 128

token_temp = 0.5
list_temp = 0.2
loss_scale = 4096.0
epsilon = 1e-06


def unit_rows(values):
    factor = lax.rsqrt(jnp.mean(values * values, axis=-1, keepdims=True) + epsilon)
    return (values * factor, factor)


def list_tables(teacher, cand_peer, cand_doc, tile_count, shards, enc_count):
    slot_count = cand_doc.shape[1]
    valid = (jnp.arange(slot_count)[None, :] // TILE < tile_count[:, None]).astype(jnp.float32)
    target = jnp.exp(teacher) * valid
    target = target / jnp.sum(target, axis=-1, keepdims=True)
    ident = cand_peer[:, :, 0] * enc_count + cand_doc
    named = ident[:, :, None] == jnp.arange(shards * enc_count, dtype=jnp.int32)[None, None, :]
    count = jnp.sum(jnp.where(named, valid[:, :, None], 0.0), axis=1)
    wanted = jnp.sum(jnp.where(named, target[:, :, None], 0.0), axis=1)
    return count, wanted


def with_collectives(
    doc_hidden, proj_weight, query_reps, teacher, cand_peer, cand_doc, tile_count, doc_len
):
    enc_count, doc_tokens, hidden_part = doc_hidden.shape
    shards = lax.axis_size("dp")
    me = lax.axis_index("dp")
    inv_root = 1.0 / math.sqrt(EMB)
    query_unit, query_factor = unit_rows(query_reps.astype(jnp.float32))
    query_narrow = query_unit.astype(jnp.bfloat16)
    count, wanted = list_tables(teacher, cand_peer, cand_doc, tile_count, shards, enc_count)
    every_query = lax.all_gather(query_narrow, "dp", axis=0, tiled=True)
    tables = lax.all_gather(jnp.stack([count, wanted], axis=1), "dp", axis=0, tiled=True)
    tables = lax.dynamic_slice_in_dim(tables, me * enc_count, enc_count, axis=2)
    count, wanted = tables[:, 0], tables[:, 1]
    flat_hidden = doc_hidden.reshape(enc_count * doc_tokens, hidden_part)
    proj_part = jnp.dot(flat_hidden, proj_weight, preferred_element_type=jnp.float32)
    doc_proj = lax.psum(proj_part, "tensor").reshape(enc_count, doc_tokens, EMB)
    doc_unit, doc_factor = unit_rows(doc_proj)
    doc_narrow = doc_unit.astype(jnp.bfloat16)
    own_len = lax.dynamic_slice_in_dim(doc_len, me * enc_count, enc_count)
    token_mask = (jnp.arange(doc_tokens)[None, :] < own_len[:, None]).astype(jnp.float32)
    similarity = (
        jnp.einsum("qid,ejd->qiej", every_query, doc_narrow, preferred_element_type=jnp.float32)
        * inv_root
    )
    weights = jnp.exp(similarity / token_temp) * token_mask
    totals = jnp.sum(weights, axis=-1)
    scores = jnp.mean(token_temp * jnp.log(totals), axis=1)
    raised = jnp.exp(scores / list_temp) * count
    norm = lax.psum(jnp.sum(raised, axis=-1), "dp")
    score_grad = loss_scale * (raised / norm[:, None] - wanted) / list_temp
    token_grad = weights / totals[..., None] * (score_grad / QT)[:, None, :, None]
    token_narrow = token_grad.astype(jnp.bfloat16)
    doc_grad = (
        jnp.einsum("qiej,qid->ejd", token_narrow, every_query, preferred_element_type=jnp.float32)
        * inv_root
    )
    query_part = (
        jnp.einsum("qiej,ejd->qid", token_narrow, doc_narrow, preferred_element_type=jnp.float32)
        * inv_root
    )
    query_sum = lax.psum_scatter(query_part, "dp", scatter_dimension=0, tiled=True)
    proj_grad = doc_factor * (
        doc_grad - doc_unit * jnp.mean(doc_unit * doc_grad, axis=-1, keepdims=True)
    )
    proj_narrow = proj_grad.astype(jnp.bfloat16).reshape(enc_count * doc_tokens, EMB)
    grad_hidden = lax.dot_general(
        proj_narrow, proj_weight, (((1,), (1,)), ((), ())), preferred_element_type=jnp.float32
    ).astype(jnp.bfloat16)
    grad_hidden = grad_hidden.reshape(enc_count, doc_tokens, hidden_part)
    weight_part = lax.dot_general(
        flat_hidden, proj_narrow, (((0,), (0,)), ((), ())), preferred_element_type=jnp.float32
    )
    grad_weight = lax.psum(weight_part, "dp") / (enc_count * shards)
    grad_query = query_factor * (
        query_sum - query_unit * jnp.mean(query_unit * query_sum, axis=-1, keepdims=True)
    )
    return (grad_hidden, grad_weight, grad_query)


TABLE = 16
HIGH = lax.Precision.HIGHEST
MESH = pl.DeviceIdType.MESH


def grid_of(shape, dim):
    return lax.broadcasted_iota(jnp.int32, shape, dim)


def exchange_kernel(
    shards,
    enc_count,
    doc_tokens,
    hidden_hbm,
    weight_hbm,
    query_ref,
    list_ref,
    length_ref,
    narrow_ref,
    gathered_ref,
    query_grad_ref,
    weight_t_ref,
    hidden,
    weight,
    unit,
    factor,
    doc_narrow,
    weights,
    totals,
    token_narrow,
    narrow_t,
    table_out,
    table_in,
    norms,
    part_out,
    part_in,
    pair_out,
    pair_in,
    chip_out,
    chip_in,
    side_out,
    side_in,
    own_sum,
    load_sem,
    table_send,
    table_recv,
    norm_send,
    norm_recv,
    part_send,
    part_recv,
    pair_send,
    pair_recv,
    chip_send,
    chip_recv,
    ring_send,
    ring_recv,
    mate_send,
    mate_recv,
    side_send,
    side_recv,
    fan_send,
    fan_recv,
):
    f32, bf16 = jnp.float32, jnp.bfloat16
    me = lax.axis_index("dp")
    core = lax.rem(me, 2)
    chip = lax.div(me, 2)
    chips = shards // 2
    mate = chip * 2 + (1 - core)
    lines = chips // 2
    line, side = lax.div(chip, 2), lax.rem(chip, 2)
    beside = (line * 2 + 1 - side) * 2 + core

    def shard_at(line_at, side_at, core_at):
        return (line_at * 2 + side_at) * 2 + core_at

    inv_root = 1.0 / math.sqrt(EMB)
    tokens, hid = hidden.shape
    lanes = shards * QT
    docs = 8
    block = docs * doc_tokens
    blocks = tokens // block
    chunk = hid // shards

    weight_copy = pltpu.make_async_copy(weight_hbm, weight, load_sem.at[blocks])
    weight_copy.start()

    def hidden_copy(b):
        rows = pl.ds(pl.multiple_of(b * block, block), block)
        return pltpu.make_async_copy(hidden_hbm.at[rows], hidden.at[rows], load_sem.at[b])

    for b in range(blocks):
        hidden_copy(b).start()

    barrier = pltpu.get_barrier_semaphore()
    for t in range(1, shards):
        pl.semaphore_signal(
            barrier, inc=1, device_id={"dp": lax.rem(me + t, shards)}, device_id_type=MESH
        )

    def remote(src, dst, send, recv, peer):
        return pltpu.make_async_remote_copy(
            src_ref=src,
            dst_ref=dst,
            send_sem=send,
            recv_sem=recv,
            device_id={"dp": peer},
            device_id_type=MESH,
        )

    query = query_ref[...].astype(f32)
    query_factor = lax.rsqrt(jnp.mean(query * query, axis=-1, keepdims=True) + epsilon)
    query_unit = query * query_factor
    slots = list_ref.shape[1]
    valid = list_ref[1:2, :]
    target = jnp.exp(list_ref[0:1, :]) * valid
    target = target / jnp.sum(target, axis=-1, keepdims=True)
    ident = list_ref[2:3, :]
    row = grid_of((8, slots), 0)
    high = target.astype(bf16).astype(f32)
    middle = (target - high).astype(bf16).astype(f32)
    low = target - high - middle
    terms = jnp.where(
        row == 0,
        valid,
        jnp.where(
            row == 1, high, jnp.where(row == 2, middle, jnp.where(row == 3, low, 0.0))
        ),
    ).astype(bf16)
    for p in range(shards):
        named = (grid_of((EMB, slots), 0) + p * EMB).astype(f32) == ident
        sums = lax.dot_general(
            terms,
            jnp.where(named, 1.0, 0.0).astype(bf16),
            (((1,), (1,)), ((), ())),
            preferred_element_type=f32,
        )
        listed = sums[0:1]
        aim = sums[1:2] + sums[2:3] + sums[3:4]
        high = aim.astype(bf16).astype(f32)
        middle = (aim - high).astype(bf16).astype(f32)
        low = aim - high - middle
        kind = grid_of((TABLE, EMB), 0)
        table = jnp.where(
            kind == 0,
            listed,
            jnp.where(
                kind == 1, high, jnp.where(kind == 2, middle, jnp.where(kind == 3, low, 0.0))
            ),
        )
        table_out[p, 0:QT] = query_unit.astype(bf16)
        table_out[p, QT : QT + TABLE] = table.astype(bf16)
    table_in[me] = table_out[me]

    pl.semaphore_wait(barrier, shards - 1)
    first = []
    for t in range(1, shards):
        peer = lax.rem(me + t, shards)
        first.append(
            remote(table_out.at[peer], table_in.at[me], table_send.at[t], table_recv.at[t], peer)
        )
    for copy in first:
        copy.start()

    weight_copy.wait()

    def project(b, carry):
        hidden_copy(b).wait()
        rows = pl.ds(pl.multiple_of(b * block, block), block)
        proj = jnp.dot(hidden[rows], weight[...], preferred_element_type=f32)
        scale = lax.rsqrt(jnp.mean(proj * proj, axis=-1, keepdims=True) + epsilon)
        values = proj * scale
        unit[rows] = values
        factor[rows] = jnp.broadcast_to(scale, values.shape)
        doc_narrow[rows] = values.astype(bf16)
        return carry

    lax.fori_loop(0, blocks, project, 0)

    for copy in first:
        copy.wait_recv()
    every = table_in[:, 0:QT].reshape(lanes, EMB)

    def score(b, carry):
        rows = pl.ds(pl.multiple_of(b * block, block), block)
        some = pl.ds(pl.multiple_of(b * docs, docs), docs)
        product = lax.dot_general(
            doc_narrow[rows], every, (((1,), (1,)), ((), ())), preferred_element_type=f32
        )
        grown = jnp.exp(product * (inv_root / token_temp)).reshape(docs, doc_tokens, lanes)
        inside = grid_of((docs, doc_tokens, lanes), 1).astype(f32) < length_ref[some][:, None, :]
        grown = jnp.where(inside, grown, 0.0)
        weights[rows] = grown.reshape(block, lanes)
        totals[some] = jnp.sum(grown, axis=1)
        return carry

    lax.fori_loop(0, blocks, score, 0)

    table = table_in[:, QT : QT + TABLE].reshape(shards * TABLE, EMB)
    place = grid_of((shards * TABLE, lanes), 0)
    wanted_place = lax.div(grid_of((shards * TABLE, lanes), 1), QT) * TABLE

    def spread(r, last):
        return lax.dot_general(
            table,
            jnp.where((place >= wanted_place + r) & (place <= wanted_place + last), 1.0, 0.0).astype(
                bf16
            ),
            (((0,), (0,)), ((), ())),
            preferred_element_type=f32,
        )[:enc_count]

    count = spread(0, 0)
    wanted = spread(1, 3)
    total = totals[...]
    same = lax.div(grid_of((lanes, lanes), 0), QT) == lax.div(grid_of((lanes, lanes), 1), QT)
    scores = jnp.dot(
        jnp.log(total),
        jnp.where(same, token_temp / QT, 0.0),
        precision=HIGH,
        preferred_element_type=f32,
    )
    raised = jnp.exp(scores / list_temp) * count
    gather = jnp.where(grid_of((lanes, EMB), 0) == grid_of((lanes, EMB), 1) * QT, 1.0, 0.0)
    norms[me] = jnp.dot(
        jnp.broadcast_to(jnp.sum(raised, axis=0, keepdims=True), (8, lanes)),
        gather,
        precision=HIGH,
        preferred_element_type=f32,
    )
    second = []
    for t in range(1, shards):
        peer = lax.rem(me + t, shards)
        second.append(remote(norms.at[me], norms.at[me], norm_send.at[t], norm_recv.at[t], peer))
    for copy in second:
        copy.start()
    for copy in second:
        copy.wait_recv()
    back = jnp.where(grid_of((EMB, lanes), 0) == lax.div(grid_of((EMB, lanes), 1), QT), 1.0, 0.0)
    norm = jnp.dot(
        jnp.sum(norms[...], axis=0), back, precision=HIGH, preferred_element_type=f32
    )[0:1]
    score_grad = loss_scale * (raised / norm - wanted) / list_temp
    totals[...] = (score_grad / QT) / total

    def backward(b, carry):
        rows = pl.ds(pl.multiple_of(b * block, block), block)
        some = pl.ds(pl.multiple_of(b * docs, docs), docs)
        grads = weights[rows].reshape(docs, doc_tokens, lanes) * totals[some][:, None, :]
        narrow = grads.reshape(block, lanes).astype(bf16)
        token_narrow[rows] = narrow
        doc_grad = jnp.dot(narrow, every, preferred_element_type=f32) * inv_root
        values = unit[rows]
        proj_grad = factor[rows] * (
            doc_grad - values * jnp.mean(values * doc_grad, axis=-1, keepdims=True)
        )
        narrow_ref[rows] = proj_grad.astype(bf16)
        narrow_t[b] = jnp.transpose(proj_grad).astype(bf16)
        return carry

    lax.fori_loop(0, blocks, backward, 0)

    def weight_part(c):
        columns = pl.ds(pl.multiple_of(c * chunk, chunk), chunk)
        total = jnp.zeros((EMB, chunk), f32)
        for b in range(blocks):
            total = total + jnp.dot(
                narrow_t[b], hidden[b * block : (b + 1) * block, columns],
                preferred_element_type=f32,
            )
        return total

    pairs = [
        remote(pair_out.at[t], pair_in.at[t], pair_send.at[t], pair_recv.at[t], mate)
        for t in range(chips)
    ]
    across = []
    sides = [
        remote(side_out.at[t], side_in.at[t], side_send.at[t], side_recv.at[t], beside)
        for t in range(lines)
    ]

    def bound_for(t):
        there = lax.rem(line + 1 + t % lines, lines)
        return there, (1 - side if t < lines else side)

    for t in range(chips + 1):
        if t < chips:
            there, at = bound_for(t)
            pair_out[t] = weight_part(shard_at(there, at, 1 - core)).astype(bf16)
            pairs[t].start()
        if t > 0:
            s = t - 1
            there, at = bound_for(s)
            part = weight_part(shard_at(there, at, core))
            pairs[s].wait_recv()
            part = part + pair_in[s].astype(f32)
            if s < lines:
                side_out[s] = part.astype(bf16)
                sides[s].start()
            else:
                k = s - lines
                sides[k].wait_recv()
                part = part + side_in[k].astype(f32)
                if k < lines - 1:
                    chip_out[k] = part.astype(bf16)
                    copy = remote(
                        chip_out.at[k],
                        chip_in.at[k],
                        chip_send.at[k],
                        chip_recv.at[k],
                        shard_at(there, side, core),
                    )
                    copy.start()
                    across.append(copy)
                else:
                    own_sum[...] = part

    def query_part(b, sums):
        rows = pl.ds(pl.multiple_of(b * block, block), block)
        return sums + lax.dot_general(
            token_narrow[rows],
            doc_narrow[rows],
            (((0,), (0,)), ((), ())),
            preferred_element_type=f32,
        )

    sums = lax.fori_loop(0, blocks, query_part, jnp.zeros((lanes, EMB), f32))
    part_out[...] = sums.reshape(shards, QT, EMB)
    third = []
    for t in range(1, shards):
        peer = lax.rem(me + t, shards)
        third.append(
            remote(part_out.at[peer], part_in.at[t], part_send.at[t], part_recv.at[t], peer)
        )
    for copy in third:
        copy.start()

    for p in range(shards):
        weight_t_ref[:, p * chunk : (p + 1) * chunk] = jnp.transpose(
            weight[p * chunk : (p + 1) * chunk]
        )

    for copy in across:
        copy.wait_recv()
    reduced = own_sum[...]
    for s in range(lines - 1):
        reduced = reduced + chip_in[s].astype(f32)
    own_rows = pl.ds(pl.multiple_of(me * chunk, chunk), chunk)
    gathered_ref[own_rows] = jnp.transpose(reduced * (1.0 / (enc_count * shards))).astype(bf16)

    def pass_on(source, send, recv, peer):
        rows = pl.ds(pl.multiple_of(source * chunk, chunk), chunk)
        copy = remote(gathered_ref.at[rows], gathered_ref.at[rows], send, recv, peer)
        copy.start()
        return copy

    ring = []
    for s in range(lines - 1):
        there = lax.rem(line + 1 + s, lines)
        ring.append(
            pass_on(me, ring_send.at[s], ring_recv.at[s], shard_at(there, side, core))
        )
    fan = [pass_on(me, fan_send.at[lines - 1], fan_recv.at[lines - 1], beside)]
    to_mate = [pass_on(me, mate_send.at[lines - 1], mate_recv.at[lines - 1], mate)]

    for copy in third:
        copy.wait_recv()
    query_sum = part_out[me]
    for t in range(1, shards):
        query_sum = query_sum + part_in[t]
    query_sum = query_sum * inv_root
    query_grad_ref[...] = query_factor * (
        query_sum - query_unit * jnp.mean(query_unit * query_sum, axis=-1, keepdims=True)
    )

    def from_beside(slot, line_at):
        fan[0 if slot == lines - 1 else slot + 1].wait_recv()
        to_mate.append(
            pass_on(
                shard_at(line_at, 1 - side, core),
                mate_send.at[lines + slot],
                mate_recv.at[lines + slot],
                mate,
            )
        )

    from_beside(lines - 1, line)
    sources = [lax.rem(line + 2 * lines - 1 - s, lines) for s in range(lines - 1)]
    for s in range(lines - 1):
        ring[s].wait_recv()
        source = shard_at(sources[s], side, core)
        fan.append(pass_on(source, fan_send.at[s], fan_recv.at[s], beside))
        to_mate.append(pass_on(source, mate_send.at[s], mate_recv.at[s], mate))
    for s in range(lines - 1):
        from_beside(s, sources[s])
    for copy in to_mate:
        copy.wait_recv()
    for copy in first + second + third + pairs + sides + across + ring + fan + to_mate:
        copy.wait_send()


def exchange(flat_hidden, proj_weight, query, lists, lengths, shards, enc_count, doc_tokens):
    tokens, hid = flat_hidden.shape
    lanes = shards * QT
    docs = 8
    block = docs * doc_tokens
    blocks = tokens // block
    chunk = hid // shards
    chips = shards // 2
    f32, bf16 = jnp.float32, jnp.bfloat16
    in_vmem = pl.BlockSpec(memory_space=pltpu.VMEM)
    in_hbm = pl.BlockSpec(memory_space=pltpu.HBM)
    dma = pltpu.SemaphoreType.DMA
    return pl.pallas_call(
        functools.partial(exchange_kernel, shards, enc_count, doc_tokens),
        out_shape=(
            jax.ShapeDtypeStruct((tokens, EMB), bf16),
            jax.ShapeDtypeStruct((hid, EMB), bf16),
            jax.ShapeDtypeStruct((QT, EMB), f32),
            jax.ShapeDtypeStruct((EMB, hid), bf16),
        ),
        in_specs=[in_hbm, in_hbm, in_vmem, in_vmem, in_vmem],
        out_specs=(in_vmem, in_vmem, in_vmem, in_vmem),
        scratch_shapes=[
            pltpu.VMEM((tokens, hid), bf16),
            pltpu.VMEM((hid, EMB), bf16),
            pltpu.VMEM((tokens, EMB), f32),
            pltpu.VMEM((tokens, EMB), f32),
            pltpu.VMEM((tokens, EMB), bf16),
            pltpu.VMEM((tokens, lanes), f32),
            pltpu.VMEM((enc_count, lanes), f32),
            pltpu.VMEM((tokens, lanes), bf16),
            pltpu.VMEM((blocks, EMB, block), bf16),
            pltpu.VMEM((shards, QT + TABLE, EMB), bf16),
            pltpu.VMEM((shards, QT + TABLE, EMB), bf16),
            pltpu.VMEM((shards, 8, EMB), f32),
            pltpu.VMEM((shards, QT, EMB), f32),
            pltpu.VMEM((shards, QT, EMB), f32),
            pltpu.VMEM((chips, EMB, chunk), bf16),
            pltpu.VMEM((chips, EMB, chunk), bf16),
            pltpu.VMEM((chips, EMB, chunk), bf16),
            pltpu.VMEM((chips, EMB, chunk), bf16),
            pltpu.VMEM((chips // 2, EMB, chunk), bf16),
            pltpu.VMEM((chips // 2, EMB, chunk), bf16),
            pltpu.VMEM((EMB, chunk), f32),
            dma((blocks + 1,)),
        ]
        + [dma((shards,))] * 6
        + [dma((chips,))] * 12,
        compiler_params=pltpu.CompilerParams(
            collective_id=0, has_side_effects=True, vmem_limit_bytes=60 * 1024 * 1024
        ),
    )(flat_hidden, proj_weight, query, lists, lengths)


def spread_kernel(narrow_ref, weight_t_ref, gathered_ref, hidden_grad_ref, weight_grad_ref):
    hidden_grad_ref[...] = jnp.dot(
        narrow_ref[...], weight_t_ref[...], preferred_element_type=jnp.float32
    ).astype(jnp.bfloat16)
    weight_grad_ref[...] = gathered_ref[...].astype(jnp.float32)


def hidden_gradient(proj_narrow, weight_t, gathered, steps=8):
    tokens = proj_narrow.shape[0]
    hid = weight_t.shape[1]
    return pl.pallas_call(
        spread_kernel,
        grid=(steps,),
        out_shape=(
            jax.ShapeDtypeStruct((tokens, hid), jnp.bfloat16),
            jax.ShapeDtypeStruct((hid, EMB), jnp.float32),
        ),
        in_specs=[
            pl.BlockSpec((tokens // steps, EMB), lambda i: (i, 0)),
            pl.BlockSpec((EMB, hid), lambda i: (0, 0)),
            pl.BlockSpec((hid // steps, EMB), lambda i: (i, 0)),
        ],
        out_specs=(
            pl.BlockSpec((tokens // steps, hid), lambda i: (i, 0)),
            pl.BlockSpec((hid // steps, EMB), lambda i: (i, 0)),
        ),
        compiler_params=pltpu.CompilerParams(vmem_limit_bytes=60 * 1024 * 1024),
    )(proj_narrow, weight_t, gathered)


def with_kernels(
    doc_hidden, proj_weight, query_reps, teacher, cand_peer, cand_doc, tile_count, doc_len
):
    enc_count, doc_tokens, hidden_part = doc_hidden.shape
    shards = lax.axis_size("dp")
    me = lax.axis_index("dp")
    slots = cand_doc.shape[1]
    valid = (jnp.arange(slots)[None, :] // TILE < tile_count[:, None]).astype(jnp.float32)
    ident = (cand_peer[:, :, 0] * EMB + cand_doc).astype(jnp.float32)
    lists = jnp.concatenate(
        [teacher, valid, ident, jnp.zeros((5, slots), jnp.float32)], axis=0
    )
    own_len = lax.dynamic_slice_in_dim(doc_len, me * enc_count, enc_count).astype(jnp.float32)
    lengths = jnp.broadcast_to(own_len[:, None], (enc_count, shards * QT))
    proj_narrow, gathered, grad_query, weight_t = exchange(
        doc_hidden.reshape(enc_count * doc_tokens, hidden_part),
        proj_weight,
        query_reps.reshape(QT, EMB),
        lists,
        lengths,
        shards,
        enc_count,
        doc_tokens,
    )
    grad_hidden, grad_weight = hidden_gradient(proj_narrow, weight_t, gathered)
    return (
        grad_hidden.reshape(enc_count, doc_tokens, hidden_part),
        grad_weight,
        grad_query.reshape(1, QT, EMB),
    )


def solution(mesh):
    plain = mesh.shape["tensor"] > 1 or mesh.shape["dp"] % 4 > 0
    placed = (
        P(("groups", "dp"), None, "tensor"),
        P("tensor", None),
        P(("groups", "dp"), None, None),
        P(("groups", "dp"), None),
        P(("groups", "dp"), None, None),
        P(("groups", "dp"), None),
        P(("groups", "dp")),
        P("groups"),
    )
    return jax.shard_map(
        with_collectives if plain else with_kernels,
        mesh=mesh,
        in_specs=placed,
        out_specs=(
            P(("groups", "dp"), None, "tensor"),
            P(("groups", "tensor"), None),
            P(("groups", "dp"), None, None),
        ),
        check_vma=False,
    )
```

```python
import functools
import math

import jax
import jax.numpy as jnp
from jax import lax
from jax.experimental import pallas as pl
from jax.experimental.pallas import tpu as pltpu
from jax.sharding import PartitionSpec as P

EMB = 128
QT = 32
TILE = 128

token_temp = 0.5
list_temp = 0.2
loss_scale = 4096.0
epsilon = 1e-06


def unit_rows(values):
    factor = lax.rsqrt(jnp.mean(values * values, axis=-1, keepdims=True) + epsilon)
    return (values * factor, factor)


def list_tables(teacher, cand_peer, cand_doc, tile_count, shards, enc_count):
    slot_count = cand_doc.shape[1]
    valid = (jnp.arange(slot_count)[None, :] // TILE < tile_count[:, None]).astype(jnp.float32)
    target = jnp.exp(teacher) * valid
    target = target / jnp.sum(target, axis=-1, keepdims=True)
    ident = cand_peer[:, :, 0] * enc_count + cand_doc
    named = ident[:, :, None] == jnp.arange(shards * enc_count, dtype=jnp.int32)[None, None, :]
    count = jnp.sum(jnp.where(named, valid[:, :, None], 0.0), axis=1)
    wanted = jnp.sum(jnp.where(named, target[:, :, None], 0.0), axis=1)
    return count, wanted


def with_collectives(
    doc_hidden, proj_weight, query_reps, teacher, cand_peer, cand_doc, tile_count, doc_len
):
    enc_count, doc_tokens, hidden_part = doc_hidden.shape
    shards = lax.axis_size("dp")
    me = lax.axis_index("dp")
    inv_root = 1.0 / math.sqrt(EMB)
    query_unit, query_factor = unit_rows(query_reps.astype(jnp.float32))
    query_narrow = query_unit.astype(jnp.bfloat16)
    count, wanted = list_tables(teacher, cand_peer, cand_doc, tile_count, shards, enc_count)
    every_query = lax.all_gather(query_narrow, "dp", axis=0, tiled=True)
    tables = lax.all_gather(jnp.stack([count, wanted], axis=1), "dp", axis=0, tiled=True)
    tables = lax.dynamic_slice_in_dim(tables, me * enc_count, enc_count, axis=2)
    count, wanted = tables[:, 0], tables[:, 1]
    flat_hidden = doc_hidden.reshape(enc_count * doc_tokens, hidden_part)
    proj_part = jnp.dot(flat_hidden, proj_weight, preferred_element_type=jnp.float32)
    doc_proj = lax.psum(proj_part, "tensor").reshape(enc_count, doc_tokens, EMB)
    doc_unit, doc_factor = unit_rows(doc_proj)
    doc_narrow = doc_unit.astype(jnp.bfloat16)
    own_len = lax.dynamic_slice_in_dim(doc_len, me * enc_count, enc_count)
    token_mask = (jnp.arange(doc_tokens)[None, :] < own_len[:, None]).astype(jnp.float32)
    similarity = (
        jnp.einsum("qid,ejd->qiej", every_query, doc_narrow, preferred_element_type=jnp.float32)
        * inv_root
    )
    weights = jnp.exp(similarity / token_temp) * token_mask
    totals = jnp.sum(weights, axis=-1)
    scores = jnp.mean(token_temp * jnp.log(totals), axis=1)
    raised = jnp.exp(scores / list_temp) * count
    norm = lax.psum(jnp.sum(raised, axis=-1), "dp")
    score_grad = loss_scale * (raised / norm[:, None] - wanted) / list_temp
    token_grad = weights / totals[..., None] * (score_grad / QT)[:, None, :, None]
    token_narrow = token_grad.astype(jnp.bfloat16)
    doc_grad = (
        jnp.einsum("qiej,qid->ejd", token_narrow, every_query, preferred_element_type=jnp.float32)
        * inv_root
    )
    query_part = (
        jnp.einsum("qiej,ejd->qid", token_narrow, doc_narrow, preferred_element_type=jnp.float32)
        * inv_root
    )
    query_sum = lax.psum_scatter(query_part, "dp", scatter_dimension=0, tiled=True)
    proj_grad = doc_factor * (
        doc_grad - doc_unit * jnp.mean(doc_unit * doc_grad, axis=-1, keepdims=True)
    )
    proj_narrow = proj_grad.astype(jnp.bfloat16).reshape(enc_count * doc_tokens, EMB)
    grad_hidden = lax.dot_general(
        proj_narrow, proj_weight, (((1,), (1,)), ((), ())), preferred_element_type=jnp.float32
    ).astype(jnp.bfloat16)
    grad_hidden = grad_hidden.reshape(enc_count, doc_tokens, hidden_part)
    weight_part = lax.dot_general(
        flat_hidden, proj_narrow, (((0,), (0,)), ((), ())), preferred_element_type=jnp.float32
    )
    grad_weight = lax.psum(weight_part, "dp") / (enc_count * shards)
    grad_query = query_factor * (
        query_sum - query_unit * jnp.mean(query_unit * query_sum, axis=-1, keepdims=True)
    )
    return (grad_hidden, grad_weight, grad_query)


TABLE = 16
HIGH = lax.Precision.HIGHEST
MESH = pl.DeviceIdType.MESH


def grid_of(shape, dim):
    return lax.broadcasted_iota(jnp.int32, shape, dim)


def exchange_kernel(
    shards,
    enc_count,
    doc_tokens,
    hidden_hbm,
    weight_hbm,
    query_ref,
    list_ref,
    length_ref,
    narrow_ref,
    gathered_ref,
    query_grad_ref,
    weight_t_ref,
    hidden,
    weight,
    unit,
    factor,
    doc_narrow,
    weights,
    totals,
    token_narrow,
    narrow_t,
    table_out,
    table_in,
    norms,
    part_out,
    part_in,
    pair_out,
    pair_in,
    chip_out,
    chip_in,
    side_out,
    side_in,
    own_sum,
    load_sem,
    table_send,
    table_recv,
    norm_send,
    norm_recv,
    part_send,
    part_recv,
    pair_send,
    pair_recv,
    chip_send,
    chip_recv,
    ring_send,
    ring_recv,
    mate_send,
    mate_recv,
    side_send,
    side_recv,
    fan_send,
    fan_recv,
):
    f32, bf16 = jnp.float32, jnp.bfloat16
    me = lax.axis_index("dp")
    core = lax.rem(me, 2)
    chip = lax.div(me, 2)
    chips = shards // 2
    mate = chip * 2 + (1 - core)
    lines = chips // 2
    line, side = lax.div(chip, 2), lax.rem(chip, 2)
    beside = (line * 2 + 1 - side) * 2 + core

    def shard_at(line_at, side_at, core_at):
        return (line_at * 2 + side_at) * 2 + core_at

    inv_root = 1.0 / math.sqrt(EMB)
    tokens, hid = hidden.shape
    lanes = shards * QT
    docs = 8
    block = docs * doc_tokens
    blocks = tokens // block
    chunk = hid // shards

    weight_copy = pltpu.make_async_copy(weight_hbm, weight, load_sem.at[blocks])
    weight_copy.start()

    def hidden_copy(b):
        rows = pl.ds(pl.multiple_of(b * block, block), block)
        return pltpu.make_async_copy(hidden_hbm.at[rows], hidden.at[rows], load_sem.at[b])

    for b in range(blocks):
        hidden_copy(b).start()

    barrier = pltpu.get_barrier_semaphore()
    for t in range(1, shards):
        pl.semaphore_signal(
            barrier, inc=1, device_id={"dp": lax.rem(me + t, shards)}, device_id_type=MESH
        )

    def remote(src, dst, send, recv, peer):
        return pltpu.make_async_remote_copy(
            src_ref=src,
            dst_ref=dst,
            send_sem=send,
            recv_sem=recv,
            device_id={"dp": peer},
            device_id_type=MESH,
        )

    query = query_ref[...].astype(f32)
    query_factor = lax.rsqrt(jnp.mean(query * query, axis=-1, keepdims=True) + epsilon)
    query_unit = query * query_factor
    slots = list_ref.shape[1]
    valid = list_ref[1:2, :]
    target = jnp.exp(list_ref[0:1, :]) * valid
    target = target / jnp.sum(target, axis=-1, keepdims=True)
    ident = list_ref[2:3, :]
    row = grid_of((8, slots), 0)
    high = target.astype(bf16).astype(f32)
    middle = (target - high).astype(bf16).astype(f32)
    low = target - high - middle
    terms = jnp.where(
        row == 0,
        valid,
        jnp.where(
            row == 1, high, jnp.where(row == 2, middle, jnp.where(row == 3, low, 0.0))
        ),
    ).astype(bf16)
    for p in range(shards):
        named = (grid_of((EMB, slots), 0) + p * EMB).astype(f32) == ident
        sums = lax.dot_general(
            terms,
            jnp.where(named, 1.0, 0.0).astype(bf16),
            (((1,), (1,)), ((), ())),
            preferred_element_type=f32,
        )
        listed = sums[0:1]
        aim = sums[1:2] + sums[2:3] + sums[3:4]
        high = aim.astype(bf16).astype(f32)
        middle = (aim - high).astype(bf16).astype(f32)
        low = aim - high - middle
        kind = grid_of((TABLE, EMB), 0)
        table = jnp.where(
            kind == 0,
            listed,
            jnp.where(
                kind == 1, high, jnp.where(kind == 2, middle, jnp.where(kind == 3, low, 0.0))
            ),
        )
        table_out[p, 0:QT] = query_unit.astype(bf16)
        table_out[p, QT : QT + TABLE] = table.astype(bf16)
    table_in[me] = table_out[me]

    pl.semaphore_wait(barrier, shards - 1)
    first = []
    for t in range(1, shards):
        peer = lax.rem(me + t, shards)
        first.append(
            remote(table_out.at[peer], table_in.at[me], table_send.at[t], table_recv.at[t], peer)
        )
    for copy in first:
        copy.start()

    weight_copy.wait()

    def project(b, carry):
        hidden_copy(b).wait()
        rows = pl.ds(pl.multiple_of(b * block, block), block)
        proj = jnp.dot(hidden[rows], weight[...], preferred_element_type=f32)
        scale = lax.rsqrt(jnp.mean(proj * proj, axis=-1, keepdims=True) + epsilon)
        values = proj * scale
        unit[rows] = values
        factor[rows] = jnp.broadcast_to(scale, values.shape)
        doc_narrow[rows] = values.astype(bf16)
        return carry

    lax.fori_loop(0, blocks, project, 0)

    for copy in first:
        copy.wait_recv()
    every = table_in[:, 0:QT].reshape(lanes, EMB)

    def score(b, carry):
        rows = pl.ds(pl.multiple_of(b * block, block), block)
        some = pl.ds(pl.multiple_of(b * docs, docs), docs)
        product = lax.dot_general(
            doc_narrow[rows], every, (((1,), (1,)), ((), ())), preferred_element_type=f32
        )
        grown = jnp.exp(product * (inv_root / token_temp)).reshape(docs, doc_tokens, lanes)
        inside = grid_of((docs, doc_tokens, lanes), 1).astype(f32) < length_ref[some][:, None, :]
        grown = jnp.where(inside, grown, 0.0)
        weights[rows] = grown.reshape(block, lanes)
        totals[some] = jnp.sum(grown, axis=1)
        return carry

    lax.fori_loop(0, blocks, score, 0)

    table = table_in[:, QT : QT + TABLE].reshape(shards * TABLE, EMB)
    place = grid_of((shards * TABLE, lanes), 0)
    wanted_place = lax.div(grid_of((shards * TABLE, lanes), 1), QT) * TABLE

    def spread(r, last):
        return lax.dot_general(
            table,
            jnp.where((place >= wanted_place + r) & (place <= wanted_place + last), 1.0, 0.0).astype(
                bf16
            ),
            (((0,), (0,)), ((), ())),
            preferred_element_type=f32,
        )[:enc_count]

    count = spread(0, 0)
    wanted = spread(1, 3)
    total = totals[...]
    same = lax.div(grid_of((lanes, lanes), 0), QT) == lax.div(grid_of((lanes, lanes), 1), QT)
    scores = jnp.dot(
        jnp.log(total),
        jnp.where(same, token_temp / QT, 0.0),
        precision=HIGH,
        preferred_element_type=f32,
    )
    raised = jnp.exp(scores / list_temp) * count
    gather = jnp.where(grid_of((lanes, EMB), 0) == grid_of((lanes, EMB), 1) * QT, 1.0, 0.0)
    norms[me] = jnp.dot(
        jnp.broadcast_to(jnp.sum(raised, axis=0, keepdims=True), (8, lanes)),
        gather,
        precision=HIGH,
        preferred_element_type=f32,
    )
    second = []
    for t in range(1, shards):
        peer = lax.rem(me + t, shards)
        second.append(remote(norms.at[me], norms.at[me], norm_send.at[t], norm_recv.at[t], peer))
    for copy in second:
        copy.start()
    for copy in second:
        copy.wait_recv()
    back = jnp.where(grid_of((EMB, lanes), 0) == lax.div(grid_of((EMB, lanes), 1), QT), 1.0, 0.0)
    norm = jnp.dot(
        jnp.sum(norms[...], axis=0), back, precision=HIGH, preferred_element_type=f32
    )[0:1]
    score_grad = loss_scale * (raised / norm - wanted) / list_temp
    totals[...] = (score_grad / QT) / total

    def backward(b, carry):
        rows = pl.ds(pl.multiple_of(b * block, block), block)
        some = pl.ds(pl.multiple_of(b * docs, docs), docs)
        grads = weights[rows].reshape(docs, doc_tokens, lanes) * totals[some][:, None, :]
        narrow = grads.reshape(block, lanes).astype(bf16)
        token_narrow[rows] = narrow
        doc_grad = jnp.dot(narrow, every, preferred_element_type=f32) * inv_root
        values = unit[rows]
        proj_grad = factor[rows] * (
            doc_grad - values * jnp.mean(values * doc_grad, axis=-1, keepdims=True)
        )
        narrow_ref[rows] = proj_grad.astype(bf16)
        narrow_t[b] = jnp.transpose(proj_grad).astype(bf16)
        return carry

    lax.fori_loop(0, blocks, backward, 0)

    def weight_part(c):
        columns = pl.ds(pl.multiple_of(c * chunk, chunk), chunk)
        total = jnp.zeros((EMB, chunk), f32)
        for b in range(blocks):
            total = total + jnp.dot(
                narrow_t[b], hidden[b * block : (b + 1) * block, columns],
                preferred_element_type=f32,
            )
        return total

    pairs = [
        remote(pair_out.at[t], pair_in.at[t], pair_send.at[t], pair_recv.at[t], mate)
        for t in range(chips)
    ]
    across = []
    sides = [
        remote(side_out.at[t], side_in.at[t], side_send.at[t], side_recv.at[t], beside)
        for t in range(lines)
    ]

    def bound_for(t):
        there = lax.rem(line + 1 + t % lines, lines)
        return there, (1 - side if t < lines else side)

    for t in range(chips + 1):
        if t < chips:
            there, at = bound_for(t)
            pair_out[t] = weight_part(shard_at(there, at, 1 - core)).astype(bf16)
            pairs[t].start()
        if t > 0:
            s = t - 1
            there, at = bound_for(s)
            part = weight_part(shard_at(there, at, core))
            pairs[s].wait_recv()
            part = part + pair_in[s].astype(f32)
            if s < lines:
                side_out[s] = part.astype(bf16)
                sides[s].start()
            else:
                k = s - lines
                sides[k].wait_recv()
                part = part + side_in[k].astype(f32)
                if k < lines - 1:
                    chip_out[k] = part.astype(bf16)
                    copy = remote(
                        chip_out.at[k],
                        chip_in.at[k],
                        chip_send.at[k],
                        chip_recv.at[k],
                        shard_at(there, side, core),
                    )
                    copy.start()
                    across.append(copy)
                else:
                    own_sum[...] = part

    def query_part(b, sums):
        rows = pl.ds(pl.multiple_of(b * block, block), block)
        return sums + lax.dot_general(
            token_narrow[rows],
            doc_narrow[rows],
            (((0,), (0,)), ((), ())),
            preferred_element_type=f32,
        )

    sums = lax.fori_loop(0, blocks, query_part, jnp.zeros((lanes, EMB), f32))
    part_out[...] = sums.reshape(shards, QT, EMB)
    third = []
    for t in range(1, shards):
        peer = lax.rem(me + t, shards)
        third.append(
            remote(part_out.at[peer], part_in.at[t], part_send.at[t], part_recv.at[t], peer)
        )
    for copy in third:
        copy.start()

    for p in range(shards):
        weight_t_ref[:, p * chunk : (p + 1) * chunk] = jnp.transpose(
            weight[p * chunk : (p + 1) * chunk]
        )

    for copy in across:
        copy.wait_recv()
    reduced = own_sum[...]
    for s in range(lines - 1):
        reduced = reduced + chip_in[s].astype(f32)
    own_rows = pl.ds(pl.multiple_of(me * chunk, chunk), chunk)
    gathered_ref[own_rows] = jnp.transpose(reduced * (1.0 / (enc_count * shards))).astype(bf16)

    def pass_on(source, send, recv, peer):
        rows = pl.ds(pl.multiple_of(source * chunk, chunk), chunk)
        copy = remote(gathered_ref.at[rows], gathered_ref.at[rows], send, recv, peer)
        copy.start()
        return copy

    ring = []
    for s in range(lines - 1):
        there = lax.rem(line + 1 + s, lines)
        ring.append(
            pass_on(me, ring_send.at[s], ring_recv.at[s], shard_at(there, side, core))
        )
    fan = [pass_on(me, fan_send.at[lines - 1], fan_recv.at[lines - 1], beside)]
    to_mate = [pass_on(me, mate_send.at[lines - 1], mate_recv.at[lines - 1], mate)]

    for copy in third:
        copy.wait_recv()
    query_sum = part_out[me]
    for t in range(1, shards):
        query_sum = query_sum + part_in[t]
    query_sum = query_sum * inv_root
    query_grad_ref[...] = query_factor * (
        query_sum - query_unit * jnp.mean(query_unit * query_sum, axis=-1, keepdims=True)
    )

    def from_beside(slot, line_at):
        fan[0 if slot == lines - 1 else slot + 1].wait_recv()
        to_mate.append(
            pass_on(
                shard_at(line_at, 1 - side, core),
                mate_send.at[lines + slot],
                mate_recv.at[lines + slot],
                mate,
            )
        )

    from_beside(lines - 1, line)
    sources = [lax.rem(line + 2 * lines - 1 - s, lines) for s in range(lines - 1)]
    for s in range(lines - 1):
        ring[s].wait_recv()
        source = shard_at(sources[s], side, core)
        fan.append(pass_on(source, fan_send.at[s], fan_recv.at[s], beside))
        to_mate.append(pass_on(source, mate_send.at[s], mate_recv.at[s], mate))
    for s in range(lines - 1):
        from_beside(s, sources[s])
    for copy in to_mate:
        copy.wait_recv()
    for copy in first + second + third + pairs + sides + across + ring + fan + to_mate:
        copy.wait_send()


def exchange(flat_hidden, proj_weight, query, lists, lengths, shards, enc_count, doc_tokens):
    tokens, hid = flat_hidden.shape
    lanes = shards * QT
    docs = 8
    block = docs * doc_tokens
    blocks = tokens // block
    chunk = hid // shards
    chips = shards // 2
    f32, bf16 = jnp.float32, jnp.bfloat16
    in_vmem = pl.BlockSpec(memory_space=pltpu.VMEM)
    in_hbm = pl.BlockSpec(memory_space=pltpu.HBM)
    dma = pltpu.SemaphoreType.DMA
    return pl.pallas_call(
        functools.partial(exchange_kernel, shards, enc_count, doc_tokens),
        out_shape=(
            jax.ShapeDtypeStruct((tokens, EMB), bf16),
            jax.ShapeDtypeStruct((hid, EMB), bf16),
            jax.ShapeDtypeStruct((QT, EMB), f32),
            jax.ShapeDtypeStruct((EMB, hid), bf16),
        ),
        in_specs=[in_hbm, in_hbm, in_vmem, in_vmem, in_vmem],
        out_specs=(in_vmem, in_vmem, in_vmem, in_vmem),
        scratch_shapes=[
            pltpu.VMEM((tokens, hid), bf16),
            pltpu.VMEM((hid, EMB), bf16),
            pltpu.VMEM((tokens, EMB), f32),
            pltpu.VMEM((tokens, EMB), f32),
            pltpu.VMEM((tokens, EMB), bf16),
            pltpu.VMEM((tokens, lanes), f32),
            pltpu.VMEM((enc_count, lanes), f32),
            pltpu.VMEM((tokens, lanes), bf16),
            pltpu.VMEM((blocks, EMB, block), bf16),
            pltpu.VMEM((shards, QT + TABLE, EMB), bf16),
            pltpu.VMEM((shards, QT + TABLE, EMB), bf16),
            pltpu.VMEM((shards, 8, EMB), f32),
            pltpu.VMEM((shards, QT, EMB), f32),
            pltpu.VMEM((shards, QT, EMB), f32),
            pltpu.VMEM((chips, EMB, chunk), bf16),
            pltpu.VMEM((chips, EMB, chunk), bf16),
            pltpu.VMEM((chips, EMB, chunk), bf16),
            pltpu.VMEM((chips, EMB, chunk), bf16),
            pltpu.VMEM((chips // 2, EMB, chunk), bf16),
            pltpu.VMEM((chips // 2, EMB, chunk), bf16),
            pltpu.VMEM((EMB, chunk), f32),
            dma((blocks + 1,)),
        ]
        + [dma((shards,))] * 6
        + [dma((chips,))] * 12,
        compiler_params=pltpu.CompilerParams(
            collective_id=0, has_side_effects=True, vmem_limit_bytes=48 * 1024 * 1024
        ),
    )(flat_hidden, proj_weight, query, lists, lengths)


def spread_kernel(narrow_ref, weight_t_ref, gathered_ref, hidden_grad_ref, weight_grad_ref):
    hidden_grad_ref[...] = jnp.dot(
        narrow_ref[...], weight_t_ref[...], preferred_element_type=jnp.float32
    ).astype(jnp.bfloat16)
    weight_grad_ref[...] = gathered_ref[...].astype(jnp.float32)


def hidden_gradient(proj_narrow, weight_t, gathered, steps=8):
    tokens = proj_narrow.shape[0]
    hid = weight_t.shape[1]
    return pl.pallas_call(
        spread_kernel,
        grid=(steps,),
        out_shape=(
            jax.ShapeDtypeStruct((tokens, hid), jnp.bfloat16),
            jax.ShapeDtypeStruct((hid, EMB), jnp.float32),
        ),
        in_specs=[
            pl.BlockSpec((tokens // steps, EMB), lambda i: (i, 0)),
            pl.BlockSpec((EMB, hid), lambda i: (0, 0)),
            pl.BlockSpec((hid // steps, EMB), lambda i: (i, 0)),
        ],
        out_specs=(
            pl.BlockSpec((tokens // steps, hid), lambda i: (i, 0)),
            pl.BlockSpec((hid // steps, EMB), lambda i: (i, 0)),
        ),
        compiler_params=pltpu.CompilerParams(vmem_limit_bytes=48 * 1024 * 1024),
    )(proj_narrow, weight_t, gathered)


def with_kernels(
    doc_hidden, proj_weight, query_reps, teacher, cand_peer, cand_doc, tile_count, doc_len
):
    enc_count, doc_tokens, hidden_part = doc_hidden.shape
    shards = lax.axis_size("dp")
    me = lax.axis_index("dp")
    slots = cand_doc.shape[1]
    valid = (jnp.arange(slots)[None, :] // TILE < tile_count[:, None]).astype(jnp.float32)
    ident = (cand_peer[:, :, 0] * EMB + cand_doc).astype(jnp.float32)
    lists = jnp.concatenate(
        [teacher, valid, ident, jnp.zeros((5, slots), jnp.float32)], axis=0
    )
    own_len = lax.dynamic_slice_in_dim(doc_len, me * enc_count, enc_count).astype(jnp.float32)
    lengths = jnp.broadcast_to(own_len[:, None], (enc_count, shards * QT))
    proj_narrow, gathered, grad_query, weight_t = exchange(
        doc_hidden.reshape(enc_count * doc_tokens, hidden_part),
        proj_weight,
        query_reps.reshape(QT, EMB),
        lists,
        lengths,
        shards,
        enc_count,
        doc_tokens,
    )
    grad_hidden, grad_weight = hidden_gradient(proj_narrow, weight_t, gathered)
    return (
        grad_hidden.reshape(enc_count, doc_tokens, hidden_part),
        grad_weight,
        grad_query.reshape(1, QT, EMB),
    )


def solution(mesh):
    plain = mesh.shape["tensor"] > 1 or mesh.shape["dp"] % 4 > 0
    placed = (
        P(("groups", "dp"), None, "tensor"),
        P("tensor", None),
        P(("groups", "dp"), None, None),
        P(("groups", "dp"), None),
        P(("groups", "dp"), None, None),
        P(("groups", "dp"), None),
        P(("groups", "dp")),
        P("groups"),
    )
    return jax.shard_map(
        with_collectives if plain else with_kernels,
        mesh=mesh,
        in_specs=placed,
        out_specs=(
            P(("groups", "dp"), None, "tensor"),
            P(("groups", "tensor"), None),
            P(("groups", "dp"), None, None),
        ),
        check_vma=False,
    )
```
